256 devices in a mesh: probe: 32 (over z_lo, y, core), strip: 8 (over z_hi, x).
Axes of the slice: x: 4, y: 4, z: 8 (z_hi: 2, z_lo: 4; z = z_hi * 4 + z_lo), core: 2. Of those that a mesh axis runs over, the one named last changes fastest.
Arguments:
- potential: float32 [2, 512, 8192], P(None, 'probe', 'strip'), may hold values from 0 to 2
- probe_wave: float32 [2, 256, 256], replicated, may hold values from -6 to 6
- offsets: int32 [8, 2, 192], P('strip'), may hold values from -128 to 896, as said below
- members: int32 [8, 32, 6], P('strip', 'probe'), may hold values from 0 to 191, as said below
- counts: int32 [8, 32], P('strip', 'probe'), may hold values from 1 to 6, as said below
- measured: float32 [8, 32, 6, 256, 256], P('strip', 'probe'), may hold values from 0 to 4
Outputs:
- potential_grad: float32 [2, 512, 8192], P(None, 'probe', 'strip')
The draws below stay inside these ranges and needn't reach their ends.
Inputs may be any that keep to these rules, and one draw needn't show every extreme that they name: offsets[s, 0, p] is a window's first row, 0 to 256; offsets[s, 1, p] its first column counted from the strip's first column, -128 to 896; both ends of both ranges occur in every strip. `members`: every position of a strip is listed exactly once over that strip's groups; a group uses its first counts[s, g] entries. `counts`: in every strip some group uses all 6 slots and some group uses one.
All inputs are finite; a program needn't handle non-finite values.
Results may differ from the reference program's by a relative error of at most 0.00021.
Values sent between devices are 32-bit elements; how exact they have to be, the bound alone decides.
A program may use at most 64 MiB of HBM per device.

```python
import jax
import jax.numpy as jnp
from jax import lax

PW = 256
NSLICE = 2
SH = 512
SW = 1024
EDGE = 128
GMAX = 6
STRIPS = 8
GROUPS = 32
POS = 192
SW_ALL = 8192


def draw_offsets(key, part):
    first_key, second_key = jax.random.split(jax.random.fold_in(key, 11))
    rows_drawn = jax.random.randint(first_key, (STRIPS, POS), 0, SH - PW + 1)
    columns_drawn = jax.random.randint(second_key, (STRIPS, POS), -EDGE, SW + EDGE - PW + 1)
    rows_drawn = rows_drawn.at[:, 0].set(0).at[:, 1].set(SH - PW)
    columns_drawn = columns_drawn.at[:, 0].set(-EDGE).at[:, 1].set(SW + EDGE - PW)
    return jnp.stack([rows_drawn, columns_drawn], axis=1).astype(jnp.int32)


def draw_members(key, part):
    strip_keys = jax.random.split(jax.random.fold_in(key, 23), STRIPS)
    orders = jax.vmap(lambda one_key: jax.random.permutation(one_key, POS))(strip_keys)
    return orders.reshape(STRIPS, GROUPS, GMAX).astype(jnp.int32)


def draw_counts(key, part):
    first_key, second_key = jax.random.split(jax.random.fold_in(key, 37))
    drawn = jax.random.randint(first_key, (STRIPS, GROUPS), 1, GMAX + 1)
    full_group = jax.random.randint(second_key, (STRIPS,), 0, GROUPS)
    single_group = (full_group + 1) % GROUPS
    group_ids = jnp.arange(GROUPS)[None, :]
    drawn = jnp.where(group_ids == single_group[:, None], 1, drawn)
    drawn = jnp.where(group_ids == full_group[:, None], GMAX, drawn)
    return drawn.astype(jnp.int32)


def block_levels(own_key, dims, cuts, least, largest):
    def one(axis_at, blocks):
        heights = jax.random.uniform(jax.random.fold_in(jax.random.fold_in(own_key, 6), axis_at), (blocks,), jnp.float32, least / len(cuts), largest / len(cuts))
        return jnp.repeat(jnp.exp(heights), dims[axis_at] // blocks).reshape((-1,) + (1,) * (len(dims) - axis_at - 1))

    factor_of = one(*cuts[0])
    for cut in cuts[1:]:
        factor_of = factor_of * one(*cut)
    return factor_of


def centred(rng, extent, spread, reach, held_as=jnp.bfloat16):
    return jnp.clip(spread * jax.random.normal(rng, extent, jnp.float32), -reach, reach).astype(held_as)


def setup_inputs(seed: int = 0) -> dict:
    key_list = jax.random.split(jax.random.key(seed), 7)
    return {
        "potential": jnp.clip(2.0 * jax.random.uniform(key_list[0], (NSLICE, SH, SW_ALL), jnp.float32) ** block_levels(key_list[0], (NSLICE, SH, SW_ALL), ((1, 32), (2, 8)), -0.2, 0.2), 0.0, 2.0),
        "probe_wave": centred(key_list[1], (2, PW, PW), 1.0, 6.0, jnp.float32),
        "offsets": draw_offsets(jax.random.fold_in(key_list[6], 71), 0),
        "members": draw_members(jax.random.fold_in(key_list[6], 71), 0),
        "counts": draw_counts(jax.random.fold_in(key_list[6], 71), 0),
        "measured": jnp.clip(4.0 * jax.random.uniform(key_list[5], (STRIPS, GROUPS, GMAX, PW, PW), jnp.float32) ** block_levels(key_list[5], (STRIPS, GROUPS, GMAX, PW, PW), ((0, 8), (1, 32)), -0.2, 0.2), 0.0, 4.0),
    }


A_PROP = 0.1
LOSS_SCALE = 0.03125

def laplace(values):
    padded = jnp.pad(values, ((1, 1), (1, 1)))
    return padded[2:, 1:-1] + padded[:-2, 1:-1] + padded[1:-1, 2:] + padded[1:-1, :-2] - 4.0 * values

def propagate(real_part, imag_part):
    term_re, term_im = (real_part, imag_part)
    out_re, out_im = (real_part, imag_part)
    for degree in range(1, 5):
        lap_re = laplace(term_re)
        lap_im = laplace(term_im)
        term_re, term_im = (-A_PROP / degree * lap_im, A_PROP / degree * lap_re)
        out_re = out_re + term_re
        out_im = out_im + term_im
    return (out_re, out_im)

def exit_wave(window, probe_wave):
    real_part, imag_part = (probe_wave[0], probe_wave[1])
    for slice_index in range(window.shape[0]):
        phases = window[slice_index]
        cosine, sine_part = (jnp.cos(phases), jnp.sin(phases))
        real_part, imag_part = (real_part * cosine - imag_part * sine_part, real_part * sine_part + imag_part * cosine)
        real_part, imag_part = propagate(real_part, imag_part)
    return (real_part, imag_part)

def slot_loss(window, probe_wave, intensity_data):
    real_part, imag_part = exit_wave(window, probe_wave)
    far_wave = jnp.fft.fft2(real_part + 1j * imag_part, norm='ortho')
    intensity = jnp.real(far_wave) ** 2 + jnp.imag(far_wave) ** 2
    return LOSS_SCALE * jnp.sum((intensity - intensity_data) ** 2)

def reference(potential, probe_wave, offsets, members, counts, measured):
    padded = jnp.pad(potential, ((0, 0), (0, 0), (EDGE, EDGE)))
    anchor = jnp.zeros((), jnp.int32)

    def visit(item, gradient):
        strip_index = (item // (GROUPS * GMAX)).astype(jnp.int32)
        group_index = (item // GMAX % GROUPS).astype(jnp.int32)
        slot_index = (item % GMAX).astype(jnp.int32)
        position = members[strip_index, group_index, slot_index]
        start_row = offsets[strip_index, 0, position].astype(jnp.int32)
        start_column = (strip_index * SW + EDGE + offsets[strip_index, 1, position]).astype(jnp.int32)
        window = lax.dynamic_slice(padded, (anchor, start_row, start_column), (NSLICE, PW, PW))
        window_grad = jax.grad(slot_loss)(window, probe_wave, measured[strip_index, group_index, slot_index])
        weight = (slot_index < counts[strip_index, group_index]).astype(jnp.float32)
        current = lax.dynamic_slice(gradient, (anchor, start_row, start_column), (NSLICE, PW, PW))
        return lax.dynamic_update_slice(gradient, current + weight * window_grad, (anchor, start_row, start_column))
    gradient = lax.fori_loop(0, STRIPS * GROUPS * GMAX, visit, jnp.zeros(padded.shape, jnp.float32))
    return gradient[:, :, EDGE:EDGE + SW_ALL]
```

```python
import functools, math
import numpy as np
import jax
import jax.numpy as jnp
from jax import lax
from jax.experimental import pallas as pl
from jax.experimental.pallas import tpu as pltpu
from jax.sharding import PartitionSpec as P
import ml_dtypes

PW = 256
LANES = 128
PAD = 8
ALPHA = 0.1
SCALE = 0.03125
R = 32


def tables():
    n = np.arange(PW)
    ang = -2.0 * np.pi / PW * ((n[:, None] * n[None, :]) % PW)
    tr, ti = np.cos(ang) / 16.0, np.sin(ang) / 16.0
    def split(x):
        hi = x.astype(np.float32).astype(ml_dtypes.bfloat16)
        lo = (x - hi.astype(np.float64)).astype(np.float32).astype(ml_dtypes.bfloat16)
        return hi, lo
    rh, rl = split(tr)
    ih, il = split(ti)
    right = np.block([[rh, ih], [-ih, rh], [rh, ih], [-ih, rh], [rl, il], [-il, rl]])
    left = np.block([[rh, -ih, rh, -ih, rl, -il], [ih, rh, ih, rh, il, rl]])
    return left.astype(ml_dtypes.bfloat16), right.astype(ml_dtypes.bfloat16)


def sincos(x):
    h = 0.5 * x
    z = h * h
    s = h * (1.0 + z * (-1 / 6 + z * (1 / 120 + z * (-1 / 5040 + z * (1 / 362880)))))
    c = 1.0 + z * (-0.5 + z * (1 / 24 + z * (-1 / 720 + z * (1 / 40320 + z * (-1 / 3628800)))))
    return 2.0 * s * c, 1.0 - 2.0 * s * s


def chunks(fn, rows=R):
    if UNROLL:
        for i in range(PW // rows):
            fn(i * rows)
    else:
        @pl.loop(0, PW // rows)
        def _(i):
            fn(i * rows)

UNROLL = True


def compute_kernel(offs_ref, members_ref, counts_ref, obj, probe, meas, left, right, grad,
                   a0, a1, b0, va, vb, e1, lhs, rhs):
    lane = lax.broadcasted_iota(jnp.int32, (R, LANES), 1)
    first, last = lane == 0, lane == LANES - 1

    zero8 = jnp.zeros((PAD, LANES), jnp.float32)
    for buf in (a0, a1, b0, va, vb):
        for c in range(2):
            for h in range(2):
                buf[c, h, 0:PAD, :] = zero8
                buf[c, h, PAD + PW:, :] = zero8
    for j in range(2):
        for t in range(grad.shape[1]):
            grad[j, t] = jnp.zeros(grad.shape[2:], jnp.float32)

    def load(buf, c, h, r0):
        return buf[c, h, pl.ds(PAD + r0, R), :]

    def store(buf, c, h, r0, v):
        buf[c, h, pl.ds(PAD + r0, R), :] = v

    def lap(v, c, r0):
        mid = [load(v, c, h, r0) for h in range(2)]
        lf = [pltpu.roll(m, 1, 1) for m in mid]
        rt = [pltpu.roll(m, LANES - 1, 1) for m in mid]
        lf = [jnp.where(first, 0.0, lf[0]), jnp.where(first, lf[0], lf[1])]
        rt = [jnp.where(last, rt[1], rt[0]), jnp.where(last, 0.0, rt[1])]
        out = []
        for h in range(2):
            up = v[c, h, pl.ds(PAD + r0 - 1, R), :]
            dn = v[c, h, pl.ds(PAD + r0 + 1, R), :]
            out.append((up + dn) + (lf[h] + rt[h]) - 4.0 * mid[h])
        return out

    def step(v, u, k, r0):
        lr, li = lap(v, 0, r0), lap(v, 1, r0)
        c = ALPHA / k
        re = [load(u, 0, h, r0) - c * li[h] for h in range(2)]
        im = [load(u, 1, h, r0) + c * lr[h] for h in range(2)]
        return re, im

    def propagate(u, final):
        seq = [(u, va, 4), (va, vb, 3), (vb, va, 2)]
        for v, out, k in seq:
            def body(r0):
                re, im = step(v, u, k, r0)
                for h in range(2):
                    store(out, 0, h, r0, re[h])
                    store(out, 1, h, r0, im[h])
            chunks(body)
        def body(r0):
            re, im = step(va, u, 1, r0)
            final(r0, re, im)
        chunks(body)

    def split(x):
        hi = x.astype(jnp.bfloat16)
        lo = (x - hi.astype(jnp.float32)).astype(jnp.bfloat16)
        return hi, lo

    def put_lhs(r0, re, im):
        for c, parts in enumerate((re, im)):
            for h in range(2):
                hi, lo = split(parts[h])
                lhs[pl.ds(r0, R), pl.ds(c * PW + h * LANES, LANES)] = hi
                lhs[pl.ds(r0, R), pl.ds((2 + c) * PW + h * LANES, LANES)] = lo

    def transform():
        y = jnp.dot(lhs[...], right[0:1024, :], preferred_element_type=jnp.float32)
        y = y + jnp.dot(lhs[:, 0:512], right[1024:, :], preferred_element_type=jnp.float32)
        for c in range(2):
            hi, lo = split(y[:, c * PW:(c + 1) * PW])
            rhs[c * PW:(c + 1) * PW, :] = hi
            rhs[(2 + c) * PW:(3 + c) * PW, :] = lo
        z = jnp.dot(left[:, 0:1024], rhs[...], preferred_element_type=jnp.float32)
        z = z + jnp.dot(left[:, 1024:], rhs[0:512, :], preferred_element_type=jnp.float32)
        return z[0:PW], z[PW:]

    def visit(k, carry):
        p = members_ref[0, k]
        r = offs_ref[0, p]
        col = offs_ref[1, p] + 128
        t0 = jnp.minimum(col // LANES, 7)
        s = col - t0 * LANES
        back = lax.rem(LANES - s + LANES, LANES)
        fwd = lax.rem(s, LANES)

        def window(j, r0):
            x = [pltpu.roll(obj[j, t0 + t, pl.ds(r + r0, R), :], back, 1) for t in range(3)]
            keep = lane < LANES - s
            return [jnp.where(keep, x[h], x[h + 1]) for h in range(2)]

        def scatter(j, r0, g):
            y = [pltpu.roll(x, fwd, 1) for x in g]
            keep = lane < s
            vals = [jnp.where(keep, 0.0, y[0]), jnp.where(keep, y[0], y[1]), jnp.where(keep, y[1], 0.0)]
            for t in range(3):
                grad[j, t0 + t, pl.ds(r + r0, R), :] += vals[t]

        def begin(r0):
            w0, w1 = window(0, r0), window(1, r0)
            for h in range(2):
                sn, cs = sincos(w0[h])
                pr = probe[0, pl.ds(r0, R), pl.ds(h * LANES, LANES)]
                pi = probe[1, pl.ds(r0, R), pl.ds(h * LANES, LANES)]
                store(a0, 0, h, r0, pr * cs - pi * sn)
                store(a0, 1, h, r0, pr * sn + pi * cs)
                sn, cs = sincos(w1[h])
                e1[0, h, pl.ds(r0, R), :] = cs
                e1[1, h, pl.ds(r0, R), :] = sn
        chunks(begin)

        def times_e1(dst):
            def f(r0, re, im):
                for h in range(2):
                    cs = e1[0, h, pl.ds(r0, R), :]
                    sn = e1[1, h, pl.ds(r0, R), :]
                    store(dst, 0, h, r0, re[h] * cs - im[h] * sn)
                    store(dst, 1, h, r0, re[h] * sn + im[h] * cs)
            return f

        propagate(a0, times_e1(a1))
        propagate(a1, put_lhs)
        far_re, far_im = transform()
        d = (4.0 * SCALE) * (far_re * far_re + far_im * far_im - meas[k])
        hr, hi = d * far_re, -(d * far_im)
        for c, x in enumerate((hr, hi)):
            hh, ll = split(x)
            lhs[:, c * PW:(c + 1) * PW] = hh
            lhs[:, (2 + c) * PW:(3 + c) * PW] = ll
        ur, ui = transform()
        for c, x in enumerate((ur, ui)):
            for h in range(2):
                b0[c, h, PAD:PAD + PW, :] = x[:, h * LANES:(h + 1) * LANES]

        def grads(j, a, r0, re, im):
            g = [-(re[h] * load(a, 1, h, r0) + im[h] * load(a, 0, h, r0)) for h in range(2)]
            scatter(j, r0, g)

        def mid(r0, re, im):
            grads(1, a1, r0, re, im)
            times_e1(b0)(r0, re, im)
        propagate(b0, mid)
        propagate(b0, functools.partial(grads, 0, a0))
        return carry

    lax.fori_loop(0, counts_ref[0, 0], visit, 0)


def compute(offsets, members, counts, obj, probe, meas, left, right):
    f32, bf = jnp.float32, jnp.bfloat16
    field = pltpu.VMEM((2, 2, PW + 2 * PAD, LANES), f32)
    smem = pl.BlockSpec(memory_space=pltpu.SMEM)
    vmem = pl.BlockSpec(memory_space=pltpu.VMEM)
    return pl.pallas_call(
        compute_kernel,
        out_shape=jax.ShapeDtypeStruct(obj.shape, f32),
        in_specs=[smem] * 3 + [vmem] * 5,
        out_specs=vmem,
        scratch_shapes=[
            field, field, field, field, field,
            pltpu.VMEM((2, 2, PW, LANES), f32),
            pltpu.VMEM((PW, 4 * PW), bf), pltpu.VMEM((4 * PW, PW), bf),
        ],
        compiler_params=pltpu.CompilerParams(vmem_limit_bytes=24 * 1024 * 1024),
        name="slots",
    )(offsets, members, counts, obj, probe, meas, left, right)
EDGE = 128
MESH = pl.DeviceIdType.MESH
ANY = pl.BlockSpec(memory_space=pl.ANY)
VM = pl.BlockSpec(memory_space=pltpu.VMEM)


class Place:
    def __init__(self):
        self.p, self.s = lax.axis_index("probe"), lax.axis_index("strip")
        self.c = self.p % 2
        self.y = (self.p // 2) % 4
        self.z = self.p // 8

    def zz(self, d):
        return (self.z, self.z + 1 - 2 * (self.z % 2), 3 - self.z, (self.z + 2) % 4)[d]

    def yy(self, d):
        return (self.y + d + 4) % 4

    def dev(self, z=None, y=None, c=None, s=None):
        z = self.z if z is None else z
        y = self.y if y is None else y
        c = self.c if c is None else c
        return (z * 8 + y * 2 + c, self.s if s is None else s)

    def partners(self):
        return ([self.dev(y=self.yy(1)), self.dev(y=self.yy(-1)), self.dev(c=1 - self.c)]
                + [self.dev(z=self.zz(d)) for d in (1, 2, 3)]
                + [self.dev(s=(self.s + 1) % 8), self.dev(s=(self.s + 7) % 8)])

    def barrier(self):
        sem = pltpu.get_barrier_semaphore()
        partners = self.partners()
        for who in partners:
            pl.semaphore_signal(sem, inc=1, device_id=who, device_id_type=MESH)
        pl.semaphore_wait(sem, len(partners))


class Copies:
    def __init__(self, send_sems, recv_sems):
        self.ss, self.rs, self.started = send_sems, recv_sems, []

    def send(self, i, src, dst, who):
        cp = pltpu.make_async_remote_copy(src_ref=src, dst_ref=dst, send_sem=self.ss.at[i], recv_sem=self.rs.at[i],
                                          device_id=who, device_id_type=MESH)
        cp.start()
        self.started.append(cp)

    def recv(self, i, dst, who):
        pltpu.make_async_remote_copy(src_ref=dst, dst_ref=dst, send_sem=self.ss.at[i], recv_sem=self.rs.at[i],
                                     device_id=who, device_id_type=MESH).wait_recv()

    def drain(self):
        for cp in self.started:
            cp.wait_send()


def gather_kernel(own, obj, pack, ss, rs, local_sem):
    at = Place()
    cps = Copies(ss, rs)
    for t in range(8):
        pack[:, 1 + t] = own[:, :, t * 128:(t + 1) * 128]
    at.barrier()
    left, right = at.dev(s=(at.s + 7) % 8), at.dev(s=(at.s + 1) % 8)
    cps.send(39, pack.at[:, 1], pack.at[:, 9], left)
    cps.send(40, pack.at[:, 8], pack.at[:, 0], right)
    cps.recv(39, pack.at[:, 9], right)
    cps.recv(40, pack.at[:, 0], left)

    @pl.when(at.s == 0)
    def _():
        pack[:, 0] = jnp.zeros((2, 16, 128), jnp.float32)

    @pl.when(at.s == 7)
    def _():
        pack[:, 9] = jnp.zeros((2, 16, 128), jnp.float32)

    def block(z, y, c, j=None):
        rows = pl.ds(pl.multiple_of((z * 8 + y * 2 + c) * 16, 16), 16)
        return obj.at[:, :, rows, :] if j is None else obj.at[j:j + 1, :, rows, :]

    up, down, sib = at.dev(y=at.yy(1)), at.dev(y=at.yy(-1)), at.dev(c=1 - at.c)
    mine = block(at.z, at.y, at.c)
    keep = pltpu.make_async_copy(pack, mine, local_sem)
    keep.start()

    def first(d):
        src, dst = (pack if d == 0 else block(at.zz(d), at.y, at.c)), block(at.zz(d), at.y, at.c)
        if d > 0:
            cps.recv(15 + d, dst, at.dev(z=at.zz(d)))
        cps.send(d, src, dst, up)
        cps.send(4 + d, src, dst, down)
        if d == 0:
            for e in (1, 2, 3):
                cps.send(15 + e, pack, mine, at.dev(z=at.zz(e)))
        cps.send(19 + d, src, dst, sib)

    def second(d):
        z = at.zz(d)
        cps.recv(d, block(z, at.yy(-1), at.c), down)
        half = block(z, at.yy(-1), at.c, 0)
        cps.send(8 + d, half, half, up)
        cps.send(23 + d, block(z, at.yy(-1), at.c), block(z, at.yy(-1), at.c), sib)
        cps.recv(4 + d, block(z, at.yy(1), at.c), up)
        half = block(z, at.yy(1), at.c, 1)
        cps.send(12 + d, half, half, down)
        cps.send(27 + d, block(z, at.yy(1), at.c), block(z, at.yy(1), at.c), sib)

    def third(d):
        z = at.zz(d)
        for j, i, who in ((0, 8, down), (1, 12, up)):
            half = block(z, at.yy(2), at.c, j)
            cps.recv(i + d, half, who)
            cps.send(31 + 4 * j + d, half, half, sib)

    first(0)
    first(1)
    second(0)
    first(2)
    second(1)
    third(0)
    first(3)
    second(2)
    third(1)
    second(3)
    third(2)
    third(3)
    for d in range(4):
        z = at.zz(d)
        cps.recv(19 + d, block(z, at.y, 1 - at.c), sib)
        cps.recv(23 + d, block(z, at.yy(-1), 1 - at.c), sib)
        cps.recv(27 + d, block(z, at.yy(1), 1 - at.c), sib)
        for j in range(2):
            cps.recv(31 + 4 * j + d, block(z, at.yy(2), 1 - at.c, j), sib)
    keep.wait()
    cps.drain()


def gather(own):
    return pl.pallas_call(
        gather_kernel,
        out_shape=jax.ShapeDtypeStruct((2, 10, 512, 128), jnp.float32),
        in_specs=[VM],
        out_specs=ANY,
        scratch_shapes=[pltpu.VMEM((2, 10, 16, 128), jnp.float32), pltpu.SemaphoreType.DMA((41,)),
                        pltpu.SemaphoreType.DMA((41,)), pltpu.SemaphoreType.DMA],
        compiler_params=pltpu.CompilerParams(collective_id=0, has_side_effects=True,
                                             vmem_limit_bytes=16 * 1024 * 1024),
        name="gather_rows",
    )(own)


def reduce_kernel(grad, out, acc, sib_in, half_in, full_in, z_in, edge_in, ss, rs, local_sems):
    at = Place()
    cps = Copies(ss, rs)
    loads = []
    order = (3, 2, 1, 0)
    for d in order:
        rows = pl.ds(at.zz(d) * 4, 4)
        cp = pltpu.make_async_copy(grad.at[:, :, rows, at.c], acc.at[:, :, rows], local_sems.at[d])
        cp.start()
        loads.append(cp)
    at.barrier()
    up, down, sib = at.dev(y=at.yy(1)), at.dev(y=at.yy(-1)), at.dev(c=1 - at.c)
    for d in order:
        rows = pl.ds(at.zz(d) * 4, 4)
        cps.send(d, grad.at[:, :, rows, 1 - at.c], sib_in.at[:, :, rows], sib)

    def first(n, d):
        z = at.zz(d)
        rows = pl.ds(z * 4, 4)
        loads[n].wait()
        cps.recv(d, sib_in.at[:, :, rows], sib)
        far = z * 4 + at.yy(2)
        acc[:, :, far] += sib_in[:, :, far]
        cps.send(4 + d, acc.at[0:1, :, far], half_in.at[d, 0:1], up)
        cps.send(8 + d, acc.at[1:2, :, far], half_in.at[d, 1:2], down)
        for e in (1, -1, 0):
            q = z * 4 + at.yy(e)
            acc[:, :, q] += sib_in[:, :, q]

    def second(d):
        z = at.zz(d)
        cps.recv(4 + d, half_in.at[d, 0:1], down)
        q = z * 4 + at.yy(1)
        acc[0, :, q] += half_in[d, 0]
        cps.send(12 + d, acc.at[:, :, q], full_in.at[d, 0], up)
        cps.recv(8 + d, half_in.at[d, 1:2], up)
        q = z * 4 + at.yy(-1)
        acc[1, :, q] += half_in[d, 1]
        cps.send(16 + d, acc.at[:, :, q], full_in.at[d, 1], down)

    def third(d):
        q = at.zz(d) * 4 + at.y
        cps.recv(12 + d, full_in.at[d, 0], down)
        cps.recv(16 + d, full_in.at[d, 1], up)
        acc[:, :, q] += full_in[d, 0] + full_in[d, 1]
        if d > 0:
            cps.send(19 + d, acc.at[:, :, q], z_in.at[d - 1], at.dev(z=at.zz(d)))

    first(0, 3)
    first(1, 2)
    second(3)
    first(2, 1)
    second(2)
    third(3)
    first(3, 0)
    second(1)
    third(2)
    second(0)
    third(1)
    third(0)
    for d in (3, 2, 1):
        cps.recv(19 + d, z_in.at[d - 1], at.dev(z=at.zz(d)))
    q = at.z * 4 + at.y
    acc[:, :, q] += (z_in[0] + z_in[1]) + z_in[2]
    left, right = at.dev(s=(at.s + 7) % 8), at.dev(s=(at.s + 1) % 8)
    cps.send(23, acc.at[:, 0, q], edge_in.at[1], left)
    cps.send(24, acc.at[:, 9, q], edge_in.at[0], right)
    for t in range(1, 7):
        out[:, :, t * 128:(t + 1) * 128] = acc[:, 1 + t, q]
    cps.recv(23, edge_in.at[1], right)
    cps.recv(24, edge_in.at[0], left)
    out[:, :, 0:128] = acc[:, 1, q] + jnp.where(at.s > 0, edge_in[0], 0.0)
    out[:, :, 896:1024] = acc[:, 8, q] + jnp.where(at.s < 7, edge_in[1], 0.0)
    cps.drain()


def reduce_rows(grad):
    f32 = jnp.float32
    return pl.pallas_call(
        reduce_kernel,
        out_shape=jax.ShapeDtypeStruct((2, 16, 1024), f32),
        in_specs=[ANY],
        out_specs=VM,
        scratch_shapes=[pltpu.VMEM((2, 10, 16, 16, 128), f32), pltpu.VMEM((2, 10, 16, 16, 128), f32),
                        pltpu.VMEM((4, 2, 10, 16, 128), f32), pltpu.VMEM((4, 2, 2, 10, 16, 128), f32),
                        pltpu.VMEM((3, 2, 10, 16, 128), f32), pltpu.VMEM((2, 2, 16, 128), f32),
                        pltpu.SemaphoreType.DMA((25,)), pltpu.SemaphoreType.DMA((25,)),
                        pltpu.SemaphoreType.DMA((4,))],
        compiler_params=pltpu.CompilerParams(collective_id=1, has_side_effects=True,
                                             vmem_limit_bytes=24 * 1024 * 1024),
        name="reduce_rows",
    )(grad)


def shards(potential, probe_wave, offsets, members, counts, measured):
    obj = gather(potential)
    left, right = tables()
    grad = compute(offsets[0], members[0], counts, obj, probe_wave, measured[0, 0], left, right)
    return reduce_rows(grad.reshape(2, 10, 16, 2, 16, 128))


def solution(mesh):
    placed = (
        P(None, "probe", "strip"),
        P(),
        P("strip", None, None),
        P("strip", "probe", None),
        P("strip", "probe"),
        P("strip", "probe", None, None, None),
    )
    return jax.shard_map(
        shards, mesh=mesh, in_specs=placed, out_specs=P(None, "probe", "strip"), check_vma=False
    )
```

```python
import functools, math
import numpy as np
import jax
import jax.numpy as jnp
from jax import lax
from jax.experimental import pallas as pl
from jax.experimental.pallas import tpu as pltpu
from jax.sharding import PartitionSpec as P
import ml_dtypes

PW = 256
LANES = 128
PAD = 8
ALPHA = 0.1
SCALE = 0.03125
GMAX = 6
NA, NB = 41, 80
R = 32


def tables():
    n = np.arange(PW)
    ang = -2.0 * np.pi / PW * ((n[:, None] * n[None, :]) % PW)
    m = n + 1
    sine = np.sqrt(2.0 / (PW + 1)) * np.sin(np.pi / (PW + 1) * ((m[:, None] * m[None, :]) % (2 * PW + 2)))
    lam = -4.0 * np.sin(np.pi * m / (2 * PW + 2)) ** 2
    z = 1j * ALPHA * (lam[:, None] + lam[None, :])
    diag = 1.0 + z * (1.0 + z / 2.0 * (1.0 + z / 3.0 * (1.0 + z / 4.0)))
    diag = np.stack([diag.real, diag.imag]).astype(np.float32)

    def split(x):
        hi = x.astype(np.float32).astype(ml_dtypes.bfloat16)
        lo = (x - hi.astype(np.float64)).astype(np.float32).astype(ml_dtypes.bfloat16)
        return hi, lo

    both = (np.exp(1j * ang) / 16.0) @ sine

    def pair(g):
        rh, rl = split(g.real)
        ih, il = split(g.imag)
        left = np.block([[rh, -ih, rh, -ih, rl, -il], [ih, rh, ih, rh, il, rl]])
        right = np.block([[rh, -ih, rh, -ih, rl, -il], [ih, rh, ih, rh, il, rl]]).T
        return left.astype(ml_dtypes.bfloat16), right.astype(ml_dtypes.bfloat16)

    sh, sl = split(sine)
    left_f, right_f = pair(both)
    left_b, right_b = pair(both.T)
    sine_left = np.concatenate([sh, sh, sl], axis=1).astype(ml_dtypes.bfloat16)
    return left_f, right_f, left_b, right_b, sine_left, np.ascontiguousarray(sine_left.T), diag


def sincos(x):
    h = 0.5 * x
    z = h * h
    s = h * (1.0 + z * (-1 / 6 + z * (1 / 120 + z * (-1 / 5040 + z * (1 / 362880)))))
    c = 1.0 + z * (-0.5 + z * (1 / 24 + z * (-1 / 720 + z * (1 / 40320 + z * (-1 / 3628800)))))
    return 2.0 * s * c, 1.0 - 2.0 * s * s


def interleave(a, b, na, nb):
    done = 0
    for i, _ in enumerate(a):
        while done * na < (i + 1) * nb and next(b, None) is not None:
            done += 1
    for _ in b:
        pass


def run(steps):
    for _ in steps:
        pass


def compute_kernel(offs_ref, members_ref, counts_ref, obj, probe, meas, left_f, right_f, left_b, right_b,
                   sine_left, sine_right, diag, grad, a0, a1, b0, va, vb, e1, lhs, rhs, lhs_s, lhs_t, rhs_s, hb):
    lane = lax.broadcasted_iota(jnp.int32, (R, LANES), 1)
    first, last = lane == 0, lane == LANES - 1

    zero8 = jnp.zeros((PAD, LANES), jnp.float32)
    for buf in (a0.at[0], a0.at[1], b0, va, vb):
        for c in range(2):
            for h in range(2):
                buf[c, h, 0:PAD, :] = zero8
                buf[c, h, PAD + PW:, :] = zero8
    for j in range(2):
        for t in range(grad.shape[1]):
            grad[j, t] = jnp.zeros(grad.shape[2:], jnp.float32)

    def load(buf, c, h, r0):
        return buf[c, h, pl.ds(PAD + r0, R), :]

    def store(buf, c, h, r0, v):
        buf[c, h, pl.ds(PAD + r0, R), :] = v

    def lap(v, c, r0):
        mid = [load(v, c, h, r0) for h in range(2)]
        lf = [pltpu.roll(m, 1, 1) for m in mid]
        rt = [pltpu.roll(m, LANES - 1, 1) for m in mid]
        lf = [jnp.where(first, 0.0, lf[0]), jnp.where(first, lf[0], lf[1])]
        rt = [jnp.where(last, rt[1], rt[0]), jnp.where(last, 0.0, rt[1])]
        out = []
        for h in range(2):
            up = v[c, h, pl.ds(PAD + r0 - 1, R), :]
            dn = v[c, h, pl.ds(PAD + r0 + 1, R), :]
            out.append((up + dn) + (lf[h] + rt[h]) - 4.0 * mid[h])
        return out

    def step(v, u, k, r0):
        lr, li = lap(v, 0, r0), lap(v, 1, r0)
        c = ALPHA / k
        re = [load(u, 0, h, r0) - c * li[h] for h in range(2)]
        im = [load(u, 1, h, r0) + c * lr[h] for h in range(2)]
        return re, im

    def propagate(u, final):
        seq = [(u, va, 4), (va, vb, 3), (vb, va, 2)]
        for v, out, k in seq:
            for r0 in range(0, PW, R):
                re, im = step(v, u, k, r0)
                for h in range(2):
                    store(out, 0, h, r0, re[h])
                    store(out, 1, h, r0, im[h])
                yield True
        for r0 in range(0, PW, R):
            re, im = step(va, u, 1, r0)
            final(r0, re, im)
            yield True

    def split(x):
        hi = x.astype(jnp.bfloat16)
        lo = (x - hi.astype(jnp.float32)).astype(jnp.bfloat16)
        return hi, lo

    def put_lhs(r0, h, re, im):
        for c, x in enumerate((re, im)):
            hi, lo = split(x)
            lhs[pl.ds(r0, R), pl.ds(c * PW + h * LANES, LANES)] = hi
            lhs[pl.ds(r0, R), pl.ds((2 + c) * PW + h * LANES, LANES)] = lo

    def put_sine(dst, r0, h, re, im):
        for c, x in enumerate((re, im)):
            hi, lo = split(x)
            dst[pl.ds(c * PW + r0, R), pl.ds(h * LANES, LANES)] = hi
            dst[pl.ds(c * PW + r0, R), pl.ds(PW + h * LANES, LANES)] = lo

    def dot(x, y):
        return jnp.dot(x, y, preferred_element_type=jnp.float32)

    def tile(x, r0, h):
        return x[r0:r0 + R, h * LANES:(h + 1) * LANES]

    def each(fn):
        for r0 in range(0, PW, R):
            for h in range(2):
                fn(r0, h)
            yield True

    def sine_both(src, out):
        for c in range(2):
            rows = pl.ds(c * PW, PW)
            y = dot(src[rows, :], sine_right[0:512, :]) + dot(src[rows, 0:PW], sine_right[512:, :])
            hi, lo = split(y)
            rhs_s[0:PW, c * PW:(c + 1) * PW] = hi
            rhs_s[PW:, c * PW:(c + 1) * PW] = lo
            yield True
        for c in range(2):
            cols = pl.ds(c * PW, PW)
            out.append(dot(sine_left[:, 0:512], rhs_s[:, cols]) + dot(sine_left[:, 512:], rhs_s[0:PW, cols]))
            yield True

    def transform(left, right, out):
        for c in range(2):
            cols = pl.ds(c * PW, PW)
            y = dot(lhs[...], right[0:1024, cols]) + dot(lhs[:, 0:512], right[1024:, cols])
            hi, lo = split(y)
            rhs[c * PW:(c + 1) * PW, :] = hi
            rhs[(2 + c) * PW:(3 + c) * PW, :] = lo
            yield True
        for c in range(2):
            rows = pl.ds(c * PW, PW)
            out.append(dot(left[rows, 0:1024], rhs[...]) + dot(left[rows, 1024:], rhs[0:512, :]))
            yield True

    def times_diag(src, put):
        def f(r0, h):
            dr, di = (diag[c, pl.ds(r0, R), pl.ds(h * LANES, LANES)] for c in range(2))
            x, y = tile(src[0], r0, h), tile(src[1], r0, h)
            put(r0, h, x * dr - y * di, x * di + y * dr)
        return each(f)

    def place(k):
        p = members_ref[0, k]
        r = offs_ref[0, p]
        col = offs_ref[1, p] + 128
        t0 = jnp.minimum(col // LANES, 7)
        return r, t0, col - t0 * LANES

    def times_e1(par, r0, h, re, im):
        cs = e1[par, 0, h, pl.ds(r0, R), :]
        sn = e1[par, 1, h, pl.ds(r0, R), :]
        return re * cs - im * sn, re * sn + im * cs

    def head(k, par):
        r, t0, s = place(k)
        back = lax.rem(LANES - s + LANES, LANES)
        keep = lane < LANES - s
        u = a0.at[par]

        def window(j, r0):
            x = [pltpu.roll(obj[j, t0 + t, pl.ds(r + r0, R), :], back, 1) for t in range(3)]
            return [jnp.where(keep, x[h], x[h + 1]) for h in range(2)]

        for r0 in range(0, PW, R):
            w0, w1 = window(0, r0), window(1, r0)
            for h in range(2):
                sn, cs = sincos(w0[h])
                pr = probe[0, pl.ds(r0, R), pl.ds(h * LANES, LANES)]
                pi = probe[1, pl.ds(r0, R), pl.ds(h * LANES, LANES)]
                store(u, 0, h, r0, pr * cs - pi * sn)
                store(u, 1, h, r0, pr * sn + pi * cs)
                sn, cs = sincos(w1[h])
                e1[par, 0, h, pl.ds(r0, R), :] = cs
                e1[par, 1, h, pl.ds(r0, R), :] = sn
            yield True

        def enter(r0, re, im):
            for h in range(2):
                x, y = times_e1(par, r0, h, re[h], im[h])
                a1[par, 0, h, pl.ds(r0, R), :] = x
                a1[par, 1, h, pl.ds(r0, R), :] = y
                put_sine(lhs_s, r0, h, x, y)

        yield from propagate(u, enter)

    def middle(k):
        x = []
        yield from sine_both(lhs_s, x)
        yield from times_diag(x, put_lhs)
        far = []
        yield from transform(left_f, right_f, far)

        def back(r0, h):
            x, y = tile(far[0], r0, h), tile(far[1], r0, h)
            d = (4.0 * SCALE) * (x * x + y * y - meas[k, pl.ds(r0, R), pl.ds(h * LANES, LANES)])
            put_lhs(r0, h, d * x, -(d * y))
        yield from each(back)
        x = []
        yield from transform(left_b, right_b, x)
        yield from times_diag(x, functools.partial(put_sine, lhs_t))
        y = []
        yield from sine_both(lhs_t, y)
        for c in range(2):
            hb[c] = y[c]
        yield True

    def tail(k, par, valid):
        r, t0, s = place(k)
        fwd = lax.rem(s, LANES)
        keep = lane < s
        u = a0.at[par]

        def scatter(j, r0, g):
            y = [pltpu.roll(jnp.where(valid, x, 0.0), fwd, 1) for x in g]
            vals = [jnp.where(keep, 0.0, y[0]), jnp.where(keep, y[0], y[1]), jnp.where(keep, y[1], 0.0)]
            for t in range(3):
                grad[j, t0 + t, pl.ds(r + r0, R), :] += vals[t]

        for r0 in range(0, PW, R):
            g = []
            for h in range(2):
                x, y = (hb[c, pl.ds(r0, R), pl.ds(h * LANES, LANES)] for c in range(2))
                g.append(-(x * a1[par, 1, h, pl.ds(r0, R), :] + y * a1[par, 0, h, pl.ds(r0, R), :]))
                x, y = times_e1(par, r0, h, x, y)
                store(b0, 0, h, r0, x)
                store(b0, 1, h, r0, y)
            scatter(1, r0, g)
            yield True

        def leave(r0, re, im):
            g = [-(re[h] * load(u, 1, h, r0) + im[h] * load(u, 0, h, r0)) for h in range(2)]
            scatter(0, r0, g)
        yield from propagate(b0, leave)

    count = counts_ref[0, 0]
    run(head(0, 0))

    def vector_work(i):
        other = lax.rem(i + 1, 2)
        yield from tail(jnp.maximum(i - 1, 0), other, i > 0)
        yield from head(jnp.minimum(i + 1, GMAX - 1), other)

    @pl.loop(0, count)
    def _(i):
        interleave(middle(i), vector_work(i), NA, NB)

    run(tail(count - 1, lax.rem(count - 1, 2), True))


def compute(offsets, members, counts, obj, probe, meas, *consts):
    f32, bf = jnp.float32, jnp.bfloat16
    field = pltpu.VMEM((2, 2, PW + 2 * PAD, LANES), f32)
    smem = pl.BlockSpec(memory_space=pltpu.SMEM)
    vmem = pl.BlockSpec(memory_space=pltpu.VMEM)
    return pl.pallas_call(
        compute_kernel,
        out_shape=jax.ShapeDtypeStruct(obj.shape, f32),
        in_specs=[smem] * 3 + [vmem] * 10,
        out_specs=vmem,
        scratch_shapes=[
            pltpu.VMEM((2, 2, 2, PW + 2 * PAD, LANES), f32), pltpu.VMEM((2, 2, 2, PW, LANES), f32), field, field, field,
            pltpu.VMEM((2, 2, 2, PW, LANES), f32),
            pltpu.VMEM((PW, 4 * PW), bf), pltpu.VMEM((4 * PW, PW), bf),
            pltpu.VMEM((2 * PW, 2 * PW), bf), pltpu.VMEM((2 * PW, 2 * PW), bf), pltpu.VMEM((2 * PW, 2 * PW), bf),
            pltpu.VMEM((2, PW, PW), f32),
        ],
        compiler_params=pltpu.CompilerParams(vmem_limit_bytes=24 * 1024 * 1024),
        name="slots",
    )(offsets, members, counts, obj, probe, meas, *consts)
EDGE = 128
MESH = pl.DeviceIdType.MESH
ANY = pl.BlockSpec(memory_space=pl.ANY)
VM = pl.BlockSpec(memory_space=pltpu.VMEM)


class Place:
    def __init__(self):
        self.p, self.s = lax.axis_index("probe"), lax.axis_index("strip")
        self.c = self.p % 2
        self.y = (self.p // 2) % 4
        self.z = self.p // 8

    def zz(self, d):
        return (self.z, self.z + 1 - 2 * (self.z % 2), 3 - self.z, (self.z + 2) % 4)[d]

    def yy(self, d):
        return (self.y + d + 4) % 4

    def dev(self, z=None, y=None, c=None, s=None):
        z = self.z if z is None else z
        y = self.y if y is None else y
        c = self.c if c is None else c
        return (z * 8 + y * 2 + c, self.s if s is None else s)

    def partners(self):
        return ([self.dev(y=self.yy(1)), self.dev(y=self.yy(-1)), self.dev(c=1 - self.c)]
                + [self.dev(z=self.zz(d)) for d in (1, 2, 3)]
                + [self.dev(s=(self.s + 1) % 8), self.dev(s=(self.s + 7) % 8)])

    def barrier(self):
        sem = pltpu.get_barrier_semaphore()
        partners = self.partners()
        for who in partners:
            pl.semaphore_signal(sem, inc=1, device_id=who, device_id_type=MESH)
        pl.semaphore_wait(sem, len(partners))


class Copies:
    def __init__(self, send_sems, recv_sems):
        self.ss, self.rs, self.started = send_sems, recv_sems, []

    def send(self, i, src, dst, who):
        cp = pltpu.make_async_remote_copy(src_ref=src, dst_ref=dst, send_sem=self.ss.at[i], recv_sem=self.rs.at[i],
                                          device_id=who, device_id_type=MESH)
        cp.start()
        self.started.append(cp)

    def recv(self, i, dst, who):
        pltpu.make_async_remote_copy(src_ref=dst, dst_ref=dst, send_sem=self.ss.at[i], recv_sem=self.rs.at[i],
                                     device_id=who, device_id_type=MESH).wait_recv()

    def drain(self):
        for cp in self.started:
            cp.wait_send()


def gather_kernel(own, obj, pack, ss, rs, local_sem):
    at = Place()
    cps = Copies(ss, rs)
    for t in range(8):
        pack[:, 1 + t] = own[:, :, t * 128:(t + 1) * 128]
    at.barrier()
    left, right = at.dev(s=(at.s + 7) % 8), at.dev(s=(at.s + 1) % 8)
    cps.send(39, pack.at[:, 1], pack.at[:, 9], left)
    cps.send(40, pack.at[:, 8], pack.at[:, 0], right)
    cps.recv(39, pack.at[:, 9], right)
    cps.recv(40, pack.at[:, 0], left)

    @pl.when(at.s == 0)
    def _():
        pack[:, 0] = jnp.zeros((2, 16, 128), jnp.float32)

    @pl.when(at.s == 7)
    def _():
        pack[:, 9] = jnp.zeros((2, 16, 128), jnp.float32)

    def block(z, y, c, j=None):
        rows = pl.ds(pl.multiple_of((z * 8 + y * 2 + c) * 16, 16), 16)
        return obj.at[:, :, rows, :] if j is None else obj.at[j:j + 1, :, rows, :]

    up, down, sib = at.dev(y=at.yy(1)), at.dev(y=at.yy(-1)), at.dev(c=1 - at.c)
    mine = block(at.z, at.y, at.c)
    keep = pltpu.make_async_copy(pack, mine, local_sem)
    keep.start()

    def first(d):
        src, dst = (pack if d == 0 else block(at.zz(d), at.y, at.c)), block(at.zz(d), at.y, at.c)
        if d > 0:
            cps.recv(15 + d, dst, at.dev(z=at.zz(d)))
        cps.send(d, src, dst, up)
        cps.send(4 + d, src, dst, down)
        if d == 0:
            for e in (1, 2, 3):
                cps.send(15 + e, pack, mine, at.dev(z=at.zz(e)))
        cps.send(19 + d, src, dst, sib)

    def second(d):
        z = at.zz(d)
        cps.recv(d, block(z, at.yy(-1), at.c), down)
        half = block(z, at.yy(-1), at.c, 0)
        cps.send(8 + d, half, half, up)
        cps.send(23 + d, block(z, at.yy(-1), at.c), block(z, at.yy(-1), at.c), sib)
        cps.recv(4 + d, block(z, at.yy(1), at.c), up)
        half = block(z, at.yy(1), at.c, 1)
        cps.send(12 + d, half, half, down)
        cps.send(27 + d, block(z, at.yy(1), at.c), block(z, at.yy(1), at.c), sib)

    def third(d):
        z = at.zz(d)
        for j, i, who in ((0, 8, down), (1, 12, up)):
            half = block(z, at.yy(2), at.c, j)
            cps.recv(i + d, half, who)
            cps.send(31 + 4 * j + d, half, half, sib)

    first(0)
    first(1)
    second(0)
    first(2)
    second(1)
    third(0)
    first(3)
    second(2)
    third(1)
    second(3)
    third(2)
    third(3)
    for d in range(4):
        z = at.zz(d)
        cps.recv(19 + d, block(z, at.y, 1 - at.c), sib)
        cps.recv(23 + d, block(z, at.yy(-1), 1 - at.c), sib)
        cps.recv(27 + d, block(z, at.yy(1), 1 - at.c), sib)
        for j in range(2):
            cps.recv(31 + 4 * j + d, block(z, at.yy(2), 1 - at.c, j), sib)
    keep.wait()
    cps.drain()


def gather(own):
    return pl.pallas_call(
        gather_kernel,
        out_shape=jax.ShapeDtypeStruct((2, 10, 512, 128), jnp.float32),
        in_specs=[VM],
        out_specs=ANY,
        scratch_shapes=[pltpu.VMEM((2, 10, 16, 128), jnp.float32), pltpu.SemaphoreType.DMA((41,)),
                        pltpu.SemaphoreType.DMA((41,)), pltpu.SemaphoreType.DMA],
        compiler_params=pltpu.CompilerParams(collective_id=0, has_side_effects=True,
                                             vmem_limit_bytes=16 * 1024 * 1024),
        name="gather_rows",
    )(own)


def reduce_kernel(grad, out, acc, sib_in, half_in, full_in, z_in, edge_in, ss, rs, local_sems):
    at = Place()
    cps = Copies(ss, rs)
    loads = []
    order = (3, 2, 1, 0)
    for d in order:
        rows = pl.ds(at.zz(d) * 4, 4)
        cp = pltpu.make_async_copy(grad.at[:, :, rows, at.c], acc.at[:, :, rows], local_sems.at[d])
        cp.start()
        loads.append(cp)
    at.barrier()
    up, down, sib = at.dev(y=at.yy(1)), at.dev(y=at.yy(-1)), at.dev(c=1 - at.c)
    for d in order:
        rows = pl.ds(at.zz(d) * 4, 4)
        cps.send(d, grad.at[:, :, rows, 1 - at.c], sib_in.at[:, :, rows], sib)

    def first(n, d):
        z = at.zz(d)
        rows = pl.ds(z * 4, 4)
        loads[n].wait()
        cps.recv(d, sib_in.at[:, :, rows], sib)
        far = z * 4 + at.yy(2)
        acc[:, :, far] += sib_in[:, :, far]
        cps.send(4 + d, acc.at[0:1, :, far], half_in.at[d, 0:1], up)
        cps.send(8 + d, acc.at[1:2, :, far], half_in.at[d, 1:2], down)
        for e in (1, -1, 0):
            q = z * 4 + at.yy(e)
            acc[:, :, q] += sib_in[:, :, q]

    def second(d):
        z = at.zz(d)
        cps.recv(4 + d, half_in.at[d, 0:1], down)
        q = z * 4 + at.yy(1)
        acc[0, :, q] += half_in[d, 0]
        cps.send(12 + d, acc.at[:, :, q], full_in.at[d, 0], up)
        cps.recv(8 + d, half_in.at[d, 1:2], up)
        q = z * 4 + at.yy(-1)
        acc[1, :, q] += half_in[d, 1]
        cps.send(16 + d, acc.at[:, :, q], full_in.at[d, 1], down)

    def third(d):
        q = at.zz(d) * 4 + at.y
        cps.recv(12 + d, full_in.at[d, 0], down)
        cps.recv(16 + d, full_in.at[d, 1], up)
        acc[:, :, q] += full_in[d, 0] + full_in[d, 1]
        if d > 0:
            cps.send(19 + d, acc.at[:, :, q], z_in.at[d - 1], at.dev(z=at.zz(d)))

    first(0, 3)
    first(1, 2)
    second(3)
    first(2, 1)
    second(2)
    third(3)
    first(3, 0)
    second(1)
    third(2)
    second(0)
    third(1)
    third(0)
    for d in (3, 2, 1):
        cps.recv(19 + d, z_in.at[d - 1], at.dev(z=at.zz(d)))
    q = at.z * 4 + at.y
    acc[:, :, q] += (z_in[0] + z_in[1]) + z_in[2]
    left, right = at.dev(s=(at.s + 7) % 8), at.dev(s=(at.s + 1) % 8)
    cps.send(23, acc.at[:, 0, q], edge_in.at[1], left)
    cps.send(24, acc.at[:, 9, q], edge_in.at[0], right)
    for t in range(1, 7):
        out[:, :, t * 128:(t + 1) * 128] = acc[:, 1 + t, q]
    cps.recv(23, edge_in.at[1], right)
    cps.recv(24, edge_in.at[0], left)
    out[:, :, 0:128] = acc[:, 1, q] + jnp.where(at.s > 0, edge_in[0], 0.0)
    out[:, :, 896:1024] = acc[:, 8, q] + jnp.where(at.s < 7, edge_in[1], 0.0)
    cps.drain()


def reduce_rows(grad):
    f32 = jnp.float32
    return pl.pallas_call(
        reduce_kernel,
        out_shape=jax.ShapeDtypeStruct((2, 16, 1024), f32),
        in_specs=[ANY],
        out_specs=VM,
        scratch_shapes=[pltpu.VMEM((2, 10, 16, 16, 128), f32), pltpu.VMEM((2, 10, 16, 16, 128), f32),
                        pltpu.VMEM((4, 2, 10, 16, 128), f32), pltpu.VMEM((4, 2, 2, 10, 16, 128), f32),
                        pltpu.VMEM((3, 2, 10, 16, 128), f32), pltpu.VMEM((2, 2, 16, 128), f32),
                        pltpu.SemaphoreType.DMA((25,)), pltpu.SemaphoreType.DMA((25,)),
                        pltpu.SemaphoreType.DMA((4,))],
        compiler_params=pltpu.CompilerParams(collective_id=1, has_side_effects=True,
                                             vmem_limit_bytes=24 * 1024 * 1024),
        name="reduce_rows",
    )(grad)


def shards(potential, probe_wave, offsets, members, counts, measured):
    obj = gather(potential)
    grad = compute(offsets[0], members[0], counts, obj, probe_wave, measured[0, 0], *tables())
    return reduce_rows(grad.reshape(2, 10, 16, 2, 16, 128))


def solution(mesh):
    placed = (
        P(None, "probe", "strip"),
        P(),
        P("strip", None, None),
        P("strip", "probe", None),
        P("strip", "probe"),
        P("strip", "probe", None, None, None),
    )
    return jax.shard_map(
        shards, mesh=mesh, in_specs=placed, out_specs=P(None, "probe", "strip"), check_vma=False
    )
```

```python
import functools, math
import numpy as np
import jax
import jax.numpy as jnp
from jax import lax
from jax.experimental import pallas as pl
from jax.experimental.pallas import tpu as pltpu
from jax.sharding import PartitionSpec as P
import ml_dtypes

PW = 256
LANES = 128
PAD = 8
ALPHA = 0.1
SCALE = 0.03125
GMAX = 6
TWO = 2 * PW
TILES = 10
EW = 0
NA, NB = 24, 80
R = 32


def tables():
    n = np.arange(PW)
    ang = -2.0 * np.pi / PW * ((n[:, None] * n[None, :]) % PW)
    m = n + 1
    sine = np.sqrt(2.0 / (PW + 1)) * np.sin(np.pi / (PW + 1) * ((m[:, None] * m[None, :]) % (2 * PW + 2)))
    lam = -4.0 * np.sin(np.pi * m / (2 * PW + 2)) ** 2
    z = 1j * ALPHA * (lam[:, None] + lam[None, :])
    diag = 1.0 + z * (1.0 + z / 2.0 * (1.0 + z / 3.0 * (1.0 + z / 4.0)))
    diag = np.stack([diag.real, diag.imag]).astype(np.float32)

    def split(x):
        hi = x.astype(np.float32).astype(ml_dtypes.bfloat16)
        lo = (x - hi.astype(np.float64)).astype(np.float32).astype(ml_dtypes.bfloat16)
        return hi, lo

    both = (np.exp(1j * ang) / 16.0) @ sine

    def pair(g):
        rh, rl = split(g.real)
        ih, il = split(g.imag)
        hi = np.block([[rh, -ih], [ih, rh]])
        lo = np.block([[rl, -il], [il, rl]])
        return [hi, lo, hi.T, lo.T]

    sh, sl = split(sine)
    blocks = pair(both) + pair(both.T) + [np.concatenate([sh, sl], axis=1)]
    return diag, np.concatenate([x.astype(ml_dtypes.bfloat16) for x in blocks], axis=0)


def sincos(x):
    h = 0.5 * x
    z = h * h
    s = h * (1.0 + z * (-1 / 6 + z * (1 / 120 + z * (-1 / 5040 + z * (1 / 362880)))))
    c = 1.0 + z * (-0.5 + z * (1 / 24 + z * (-1 / 720 + z * (1 / 40320 + z * (-1 / 3628800)))))
    return 2.0 * s * c, 1.0 - 2.0 * s * s


def interleave(a, b, na, nb):
    done = units = 0
    for weight in a:
        units += weight
        while done * na < units * nb and next(b, None) is not None:
            done += 1
    for _ in b:
        pass


def run(steps):
    for _ in steps:
        pass


def compute_kernel(offs_ref, members_ref, counts_ref, obj, probe, meas, diag, table, grad,
                   a0, a1, b0, va, vb, e1, lhs, rhs, lhs_s, lhs_t, rhs_s, hb):
    lane = lax.broadcasted_iota(jnp.int32, (R, LANES), 1)
    first, last = lane == 0, lane == LANES - 1

    zero8 = jnp.zeros((PAD, LANES), jnp.float32)
    for buf in (a0.at[0], a0.at[1], b0, va, vb):
        for c in range(2):
            for h in range(2):
                buf[c, h, 0:PAD, :] = zero8
                buf[c, h, PAD + PW:, :] = zero8
    for j in range(2):
        for t in range(grad.shape[1]):
            grad[j, t] = jnp.zeros(grad.shape[2:], jnp.float32)

    def load(buf, c, h, r0):
        return buf[c, h, pl.ds(PAD + r0, R), :]

    def store(buf, c, h, r0, v):
        buf[c, h, pl.ds(PAD + r0, R), :] = v

    def lap(v, c, r0):
        mid = [load(v, c, h, r0) for h in range(2)]
        lf = [pltpu.roll(m, 1, 1) for m in mid]
        rt = [pltpu.roll(m, LANES - 1, 1) for m in mid]
        lf = [jnp.where(first, 0.0, lf[0]), jnp.where(first, lf[0], lf[1])]
        rt = [jnp.where(last, rt[1], rt[0]), jnp.where(last, 0.0, rt[1])]
        out = []
        for h in range(2):
            up = v[c, h, pl.ds(PAD + r0 - 1, R), :]
            dn = v[c, h, pl.ds(PAD + r0 + 1, R), :]
            out.append((up + dn) + (lf[h] + rt[h]) - 4.0 * mid[h])
        return out

    def step(v, u, k, r0):
        lr, li = lap(v, 0, r0), lap(v, 1, r0)
        c = ALPHA / k
        re = [load(u, 0, h, r0) - c * li[h] for h in range(2)]
        im = [load(u, 1, h, r0) + c * lr[h] for h in range(2)]
        return re, im

    def propagate(u, final):
        seq = [(u, va, 4), (va, vb, 3), (vb, va, 2)]
        for v, out, k in seq:
            for r0 in range(0, PW, R):
                re, im = step(v, u, k, r0)
                for h in range(2):
                    store(out, 0, h, r0, re[h])
                    store(out, 1, h, r0, im[h])
                yield True
        for r0 in range(0, PW, R):
            re, im = step(va, u, 1, r0)
            final(r0, re, im)
            yield True

    def split(x):
        hi = x.astype(jnp.bfloat16)
        lo = (x - hi.astype(jnp.float32)).astype(jnp.bfloat16)
        return hi, lo

    def put_lhs(r0, h, re, im):
        for c, x in enumerate((re, im)):
            hi, lo = split(x)
            lhs[pl.ds(r0, R), pl.ds(c * PW + h * LANES, LANES)] = hi
            lhs[pl.ds(r0, R), pl.ds((2 + c) * PW + h * LANES, LANES)] = lo

    def put_sine(dst, r0, h, re, im):
        for c, x in enumerate((re, im)):
            hi, lo = split(x)
            dst[pl.ds(c * PW + r0, R), pl.ds(h * LANES, LANES)] = hi
            dst[pl.ds(c * PW + r0, R), pl.ds(PW + h * LANES, LANES)] = lo

    def dot(x, y):
        return jnp.dot(x, y, preferred_element_type=jnp.float32)

    def tile(x, r0, h):
        return x[r0:r0 + R, h * LANES:(h + 1) * LANES]

    def each(fn):
        for r0 in range(0, PW, R):
            for h in range(2):
                fn(r0, h)
            yield EW

    def sine_both(src, out):
        shi, slo = table[8 * TWO:, 0:PW], table[8 * TWO:, PW:]
        for c in range(2):
            rows = pl.ds(c * PW, PW)
            y = dot(src[rows, 0:PW], shi) + dot(src[rows, PW:], shi) + dot(src[rows, 0:PW], slo)
            hi, lo = split(y)
            rhs_s[0:PW, c * PW:(c + 1) * PW] = hi
            rhs_s[PW:, c * PW:(c + 1) * PW] = lo
            yield 1
        for c in range(2):
            cols = pl.ds(c * PW, PW)
            hi, lo = rhs_s[0:PW, cols], rhs_s[PW:, cols]
            out.append(dot(shi, hi) + dot(shi, lo) + dot(slo, hi))
            yield 1

    def transform(way, out):
        base = 4 * TWO * way
        for c in range(2):
            cols = pl.ds(c * PW, PW)
            hi, lo = table[pl.ds(base + 2 * TWO, TWO), cols], table[pl.ds(base + 3 * TWO, TWO), cols]
            y = dot(lhs[:, 0:TWO], hi) + dot(lhs[:, TWO:], hi) + dot(lhs[:, 0:TWO], lo)
            hi, lo = split(y)
            rhs[c * PW:(c + 1) * PW, :] = hi
            rhs[(2 + c) * PW:(3 + c) * PW, :] = lo
            yield 2
        for c in range(2):
            hi, lo = table[pl.ds(base + c * PW, PW), :], table[pl.ds(base + TWO + c * PW, PW), :]
            out.append(dot(hi, rhs[0:TWO, :]) + dot(hi, rhs[TWO:, :]) + dot(lo, rhs[0:TWO, :]))
            yield 2

    def times_diag(src, put):
        def f(r0, h):
            dr, di = (diag[c, pl.ds(r0, R), pl.ds(h * LANES, LANES)] for c in range(2))
            x, y = tile(src[0], r0, h), tile(src[1], r0, h)
            put(r0, h, x * dr - y * di, x * di + y * dr)
        return each(f)

    def place(k):
        p = members_ref[0, k]
        r = offs_ref[0, p]
        col = offs_ref[1, p]
        col = jnp.where(col < 0, col + TILES * LANES, col)
        t0 = col // LANES
        return r, [lax.rem(t0 + t, TILES) for t in range(3)], col - t0 * LANES

    def times_e1(par, r0, h, re, im):
        cs = e1[par, 0, h, pl.ds(r0, R), :]
        sn = e1[par, 1, h, pl.ds(r0, R), :]
        return re * cs - im * sn, re * sn + im * cs

    def head(k, par):
        r, tiles, s = place(k)
        back = lax.rem(LANES - s + LANES, LANES)
        keep = lane < LANES - s
        u = a0.at[par]

        def window(j, r0):
            x = [pltpu.roll(obj[j, tiles[t], pl.ds(r + r0, R), :], back, 1) for t in range(3)]
            return [jnp.where(keep, x[h], x[h + 1]) for h in range(2)]

        for r0 in range(0, PW, R):
            w0, w1 = window(0, r0), window(1, r0)
            for h in range(2):
                sn, cs = sincos(w0[h])
                pr = probe[0, pl.ds(r0, R), pl.ds(h * LANES, LANES)]
                pi = probe[1, pl.ds(r0, R), pl.ds(h * LANES, LANES)]
                store(u, 0, h, r0, pr * cs - pi * sn)
                store(u, 1, h, r0, pr * sn + pi * cs)
                sn, cs = sincos(w1[h])
                e1[par, 0, h, pl.ds(r0, R), :] = cs
                e1[par, 1, h, pl.ds(r0, R), :] = sn
            yield True

        def enter(r0, re, im):
            for h in range(2):
                x, y = times_e1(par, r0, h, re[h], im[h])
                a1[par, 0, h, pl.ds(r0, R), :] = x
                a1[par, 1, h, pl.ds(r0, R), :] = y
                put_sine(lhs_s, r0, h, x, y)

        yield from propagate(u, enter)

    def middle(k):
        x = []
        yield from sine_both(lhs_s, x)
        yield from times_diag(x, put_lhs)
        far = []
        yield from transform(0, far)

        def back(r0, h):
            x, y = tile(far[0], r0, h), tile(far[1], r0, h)
            d = (4.0 * SCALE) * (x * x + y * y - meas[k, pl.ds(r0, R), pl.ds(h * LANES, LANES)])
            put_lhs(r0, h, d * x, -(d * y))
        yield from each(back)
        x = []
        yield from transform(1, x)
        yield from times_diag(x, functools.partial(put_sine, lhs_t))
        y = []
        yield from sine_both(lhs_t, y)
        for c in range(2):
            hb[c] = y[c]
        yield 0

    def tail(k, par, valid):
        r, tiles, s = place(k)
        fwd = lax.rem(s, LANES)
        keep = lane < s
        u = a0.at[par]

        def scatter(j, r0, g):
            y = [pltpu.roll(jnp.where(valid, x, 0.0), fwd, 1) for x in g]
            vals = [jnp.where(keep, 0.0, y[0]), jnp.where(keep, y[0], y[1]), jnp.where(keep, y[1], 0.0)]
            for t in range(3):
                grad[j, tiles[t], pl.ds(r + r0, R), :] += vals[t]

        for r0 in range(0, PW, R):
            g = []
            for h in range(2):
                x, y = (hb[c, pl.ds(r0, R), pl.ds(h * LANES, LANES)] for c in range(2))
                g.append(-(x * a1[par, 1, h, pl.ds(r0, R), :] + y * a1[par, 0, h, pl.ds(r0, R), :]))
                x, y = times_e1(par, r0, h, x, y)
                store(b0, 0, h, r0, x)
                store(b0, 1, h, r0, y)
            scatter(1, r0, g)
            yield True

        def leave(r0, re, im):
            g = [-(re[h] * load(u, 1, h, r0) + im[h] * load(u, 0, h, r0)) for h in range(2)]
            scatter(0, r0, g)
        yield from propagate(b0, leave)

    count = counts_ref[0, 0]
    run(head(0, 0))

    def vector_work(i):
        other = lax.rem(i + 1, 2)
        yield from tail(jnp.maximum(i - 1, 0), other, i > 0)
        yield from head(jnp.minimum(i + 1, GMAX - 1), other)

    @pl.loop(0, count)
    def _(i):
        interleave(middle(i), vector_work(i), NA, NB)

    run(tail(count - 1, lax.rem(count - 1, 2), True))


def compute(offsets, members, counts, obj, probe, meas, *consts):
    f32, bf = jnp.float32, jnp.bfloat16
    field = pltpu.VMEM((2, 2, PW + 2 * PAD, LANES), f32)
    smem = pl.BlockSpec(memory_space=pltpu.SMEM)
    vmem = pl.BlockSpec(memory_space=pltpu.VMEM)
    return pl.pallas_call(
        compute_kernel,
        out_shape=jax.ShapeDtypeStruct(obj.shape, f32),
        in_specs=[smem] * 3 + [vmem] * 5,
        out_specs=vmem,
        scratch_shapes=[
            pltpu.VMEM((2, 2, 2, PW + 2 * PAD, LANES), f32), pltpu.VMEM((2, 2, 2, PW, LANES), f32), field, field, field,
            pltpu.VMEM((2, 2, 2, PW, LANES), f32),
            pltpu.VMEM((PW, 4 * PW), bf), pltpu.VMEM((4 * PW, PW), bf),
            pltpu.VMEM((2 * PW, 2 * PW), bf), pltpu.VMEM((2 * PW, 2 * PW), bf), pltpu.VMEM((2 * PW, 2 * PW), bf),
            pltpu.VMEM((2, PW, PW), f32),
        ],
        compiler_params=pltpu.CompilerParams(vmem_limit_bytes=24 * 1024 * 1024),
        name="slots",
    )(offsets, members, counts, obj, probe, meas, *consts)
EDGE = 128
MESH = pl.DeviceIdType.MESH
ANY = pl.BlockSpec(memory_space=pl.ANY)
VM = pl.BlockSpec(memory_space=pltpu.VMEM)


class Place:
    def __init__(self):
        self.p, self.s = lax.axis_index("probe"), lax.axis_index("strip")
        self.c = self.p % 2
        self.y = (self.p // 2) % 4
        self.z = self.p // 8

    def zz(self, d):
        return (self.z, self.z + 1 - 2 * (self.z % 2), 3 - self.z, (self.z + 2) % 4)[d]

    def yy(self, d):
        return (self.y + d + 4) % 4

    def dev(self, z=None, y=None, c=None, s=None):
        z = self.z if z is None else z
        y = self.y if y is None else y
        c = self.c if c is None else c
        return (z * 8 + y * 2 + c, self.s if s is None else s)

    def partners(self):
        return ([self.dev(y=self.yy(1)), self.dev(y=self.yy(-1)), self.dev(c=1 - self.c)]
                + [self.dev(z=self.zz(d)) for d in (1, 2, 3)]
                + [self.dev(s=(self.s + 1) % 8), self.dev(s=(self.s + 7) % 8)])

    def barrier(self):
        sem = pltpu.get_barrier_semaphore()
        partners = self.partners()
        for who in partners:
            pl.semaphore_signal(sem, inc=1, device_id=who, device_id_type=MESH)
        pl.semaphore_wait(sem, len(partners))


class Copies:
    def __init__(self, send_sems, recv_sems):
        self.ss, self.rs, self.started = send_sems, recv_sems, []

    def send(self, i, src, dst, who):
        cp = pltpu.make_async_remote_copy(src_ref=src, dst_ref=dst, send_sem=self.ss.at[i], recv_sem=self.rs.at[i],
                                          device_id=who, device_id_type=MESH)
        cp.start()
        self.started.append(cp)

    def recv(self, i, dst, who):
        pltpu.make_async_remote_copy(src_ref=dst, dst_ref=dst, send_sem=self.ss.at[i], recv_sem=self.rs.at[i],
                                     device_id=who, device_id_type=MESH).wait_recv()

    def drain(self):
        for cp in self.started:
            cp.wait_send()


MAIN, EDGES = pl.ds(0, 8), pl.ds(8, 2)


def gather_kernel(own, obj, pack, ss, rs, local_sems):
    at = Place()
    cps = Copies(ss, rs)
    tiles_in = [pltpu.make_async_copy(own.at[:, :, pl.ds(t * 128, 128)], pack.at[:, t, 0], local_sems.at[2 + t])
                for t in range(8)]
    for cp in tiles_in:
        cp.start()
    at.barrier()
    for cp in tiles_in:
        cp.wait()
    left, right = at.dev(s=(at.s + 7) % 8), at.dev(s=(at.s + 1) % 8)
    up, down, sib = at.dev(y=at.yy(1)), at.dev(y=at.yy(-1)), at.dev(c=1 - at.c)
    cps.send(53, pack.at[:, 0], pack.at[:, 8], left)
    cps.send(54, pack.at[:, 7], pack.at[:, 9], right)

    def block(n, y, c, j=None):
        js = pl.ds(0, 2) if j is None else pl.ds(j, 1)
        return obj.at[js, EDGES, pl.ds(0, 4), y, c] if n == 4 else obj.at[js, MAIN, pl.ds(at.zz(n), 1), y, c]

    def keep(i, tiles):
        cp = pltpu.make_async_copy(pack.at[:, tiles], obj.at[:, tiles, pl.ds(at.z, 1), at.y, at.c], local_sems.at[i])
        cp.start()
        return cp

    def to_z(i, tiles):
        for e in (1, 2, 3):
            cps.send(i + e, pack.at[:, tiles], obj.at[:, tiles, pl.ds(at.z, 1), at.y, at.c], at.dev(z=at.zz(e)))

    def first(n):
        dst = block(n, at.y, at.c)
        src = pack.at[:, MAIN] if n == 0 else dst
        if 0 < n < 4:
            cps.recv(45 + n, dst, at.dev(z=at.zz(n)))
        if n == 4:
            for e in (1, 2, 3):
                cps.recv(49 + e, obj.at[:, EDGES, pl.ds(at.zz(e), 1), at.y, at.c], at.dev(z=at.zz(e)))
        cps.send(n, src, dst, up)
        cps.send(5 + n, src, dst, down)
        if n == 0:
            to_z(45, MAIN)
        cps.send(20 + n, src, dst, sib)

    def second(n):
        for i, j, here, there in ((0, 0, down, up), (1, 1, up, down)):
            y = at.yy(2 * i - 1)
            got = block(n, y, at.c)
            cps.recv(5 * i + n, got, here)
            half = block(n, y, at.c, j)
            cps.send(10 + 5 * i + n, half, half, there)
            cps.send(25 + 5 * i + n, got, got, sib)

    def third(n):
        for j, who in ((0, down), (1, up)):
            half = block(n, at.yy(2), at.c, j)
            cps.recv(10 + 5 * j + n, half, who)
            cps.send(35 + 5 * j + n, half, half, sib)

    first(0)
    kept = keep(0, MAIN)
    cps.recv(53, pack.at[:, 8], right)
    cps.recv(54, pack.at[:, 9], left)

    @pl.when(at.s == 7)
    def _():
        pack[:, 8, 0] = jnp.zeros((2, 16, 128), jnp.float32)

    @pl.when(at.s == 0)
    def _():
        pack[:, 9, 0] = jnp.zeros((2, 16, 128), jnp.float32)

    to_z(49, EDGES)
    kept_edges = keep(1, EDGES)
    first(1)
    second(0)
    first(2)
    second(1)
    third(0)
    kept_edges.wait()
    first(4)
    first(3)
    second(2)
    third(1)
    second(4)
    second(3)
    third(2)
    third(4)
    third(3)
    for n in range(5):
        cps.recv(20 + n, block(n, at.y, 1 - at.c), sib)
        cps.recv(25 + n, block(n, at.yy(-1), 1 - at.c), sib)
        cps.recv(30 + n, block(n, at.yy(1), 1 - at.c), sib)
        for j in range(2):
            cps.recv(35 + 5 * j + n, block(n, at.yy(2), 1 - at.c, j), sib)
    kept.wait()
    cps.drain()


def gather(own):
    return pl.pallas_call(
        gather_kernel,
        out_shape=jax.ShapeDtypeStruct((2, 10, 4, 4, 2, 16, 128), jnp.float32),
        in_specs=[ANY],
        out_specs=ANY,
        scratch_shapes=[pltpu.VMEM((2, 10, 1, 16, 128), jnp.float32), pltpu.SemaphoreType.DMA((55,)),
                        pltpu.SemaphoreType.DMA((55,)), pltpu.SemaphoreType.DMA((10,))],
        compiler_params=pltpu.CompilerParams(collective_id=0, has_side_effects=True,
                                             vmem_limit_bytes=16 * 1024 * 1024),
        name="gather_rows",
    )(own)


def reduce_kernel(grad, out, acc, sib_in, half_in, half_e, full_in, full_e, z_in, z_e, edge_in, ss, rs, local_sems):
    at = Place()
    cps = Copies(ss, rs)
    order = (4, 3, 2, 1, 0)

    def span(n):
        return (EDGES, pl.ds(0, 4)) if n == 4 else (MAIN, pl.ds(at.zz(n), 1))

    loads = {}
    for n in order:
        ts, zs = span(n)
        loads[n] = pltpu.make_async_copy(grad.at[:, ts, zs, :, at.c], acc.at[:, ts, zs], local_sems.at[n])
        loads[n].start()
    at.barrier()
    up, down, sib = at.dev(y=at.yy(1)), at.dev(y=at.yy(-1)), at.dev(c=1 - at.c)
    left, right = at.dev(s=(at.s + 7) % 8), at.dev(s=(at.s + 1) % 8)
    for n in order:
        ts, zs = span(n)
        cps.send(n, grad.at[:, ts, zs, :, 1 - at.c], sib_in.at[:, ts, zs], sib)

    def halves(n, j):
        return half_e.at[pl.ds(j, 1)] if n == 4 else half_in.at[n, pl.ds(j, 1)]

    def fulls(n, i):
        return full_e.at[i] if n == 4 else full_in.at[n, i]

    def first(n):
        ts, zs = span(n)
        loads[n].wait()
        cps.recv(n, sib_in.at[:, ts, zs], sib)
        y = at.yy(2)
        acc[:, ts, zs, y] += sib_in[:, ts, zs, y]
        cps.send(5 + n, acc.at[0:1, ts, zs, y], halves(n, 0), up)
        cps.send(10 + n, acc.at[1:2, ts, zs, y], halves(n, 1), down)
        for e in (1, -1, 0):
            y = at.yy(e)
            acc[:, ts, zs, y] += sib_in[:, ts, zs, y]

    def second(n):
        ts, zs = span(n)
        for j, e, here, there in ((0, 1, down, up), (1, -1, up, down)):
            cps.recv(5 + 5 * j + n, halves(n, j), here)
            y = at.yy(e)
            acc[j:j + 1, ts, zs, y] += halves(n, j)[...]
            cps.send(15 + 5 * j + n, acc.at[:, ts, zs, y], fulls(n, j), there)

    def third(n):
        ts, zs = span(n)
        cps.recv(15 + n, fulls(n, 0), down)
        cps.recv(20 + n, fulls(n, 1), up)
        acc[:, ts, zs, at.y] += fulls(n, 0)[...] + fulls(n, 1)[...]
        for e in (1, 2, 3):
            if n == 4:
                cps.send(28 + e, acc.at[:, EDGES, at.zz(e), at.y], z_e.at[e - 1], at.dev(z=at.zz(e)))
            elif n == e:
                cps.send(24 + e, acc.at[:, MAIN, at.zz(e), at.y], z_in.at[e - 1], at.dev(z=at.zz(e)))

    def edges():
        for e in (1, 2, 3):
            cps.recv(28 + e, z_e.at[e - 1], at.dev(z=at.zz(e)))
        acc[:, EDGES, at.z, at.y] += (z_e[0] + z_e[1]) + z_e[2]
        cps.send(32, acc.at[:, 8, at.z, at.y], edge_in.at[0], right)
        cps.send(33, acc.at[:, 9, at.z, at.y], edge_in.at[1], left)

    first(4)
    first(3)
    second(4)
    first(2)
    second(3)
    third(4)
    first(1)
    second(2)
    third(3)
    edges()
    first(0)
    second(1)
    third(2)
    second(0)
    third(1)
    cps.recv(32, edge_in.at[0], left)
    cps.recv(33, edge_in.at[1], right)
    third(0)
    for e in (3, 2, 1):
        cps.recv(24 + e, z_in.at[e - 1], at.dev(z=at.zz(e)))
    for t in range(8):
        value = acc[:, t, at.z, at.y] + ((z_in[0, :, t] + z_in[1, :, t]) + z_in[2, :, t])
        if t == 0:
            value = value + jnp.where(at.s > 0, edge_in[0], 0.0)
        if t == 7:
            value = value + jnp.where(at.s < 7, edge_in[1], 0.0)
        out[:, :, t * 128:(t + 1) * 128] = value
    cps.drain()


def reduce_rows(grad):
    f32 = jnp.float32
    return pl.pallas_call(
        reduce_kernel,
        out_shape=jax.ShapeDtypeStruct((2, 16, 1024), f32),
        in_specs=[ANY],
        out_specs=VM,
        scratch_shapes=[pltpu.VMEM((2, 10, 4, 4, 16, 128), f32), pltpu.VMEM((2, 10, 4, 4, 16, 128), f32),
                        pltpu.VMEM((4, 2, 8, 1, 16, 128), f32), pltpu.VMEM((2, 2, 4, 16, 128), f32),
                        pltpu.VMEM((4, 2, 2, 8, 1, 16, 128), f32), pltpu.VMEM((2, 2, 2, 4, 16, 128), f32),
                        pltpu.VMEM((3, 2, 8, 16, 128), f32), pltpu.VMEM((3, 2, 2, 16, 128), f32),
                        pltpu.VMEM((2, 2, 16, 128), f32),
                        pltpu.SemaphoreType.DMA((34,)), pltpu.SemaphoreType.DMA((34,)),
                        pltpu.SemaphoreType.DMA((5,))],
        compiler_params=pltpu.CompilerParams(collective_id=1, has_side_effects=True,
                                             vmem_limit_bytes=24 * 1024 * 1024),
        name="reduce_rows",
    )(grad)


def shards(potential, probe_wave, offsets, members, counts, measured):
    obj = gather(potential).reshape(2, 10, 512, 128)
    grad = compute(offsets[0], members[0], counts, obj, probe_wave, measured[0, 0], *tables())
    return reduce_rows(grad.reshape(2, 10, 4, 4, 2, 16, 128))


def solution(mesh):
    placed = (
        P(None, "probe", "strip"),
        P(),
        P("strip", None, None),
        P("strip", "probe", None),
        P("strip", "probe"),
        P("strip", "probe", None, None, None),
    )
    return jax.shard_map(
        shards, mesh=mesh, in_specs=placed, out_specs=P(None, "probe", "strip"), check_vma=False
    )
```

```python
import functools, math
import numpy as np
import jax
import jax.numpy as jnp
from jax import lax
from jax.experimental import pallas as pl
from jax.experimental.pallas import tpu as pltpu
from jax.sharding import PartitionSpec as P
import ml_dtypes

PW = 256
LANES = 128
PAD = 8
ALPHA = 0.1
SCALE = 0.03125
GMAX = 6
TWO = 2 * PW
TILES = 10
EW = 0
NA, NB = 24, 80
R = 32


def tables():
    n = np.arange(PW)
    ang = -2.0 * np.pi / PW * ((n[:, None] * n[None, :]) % PW)
    m = n + 1
    sine = np.sqrt(2.0 / (PW + 1)) * np.sin(np.pi / (PW + 1) * ((m[:, None] * m[None, :]) % (2 * PW + 2)))
    lam = -4.0 * np.sin(np.pi * m / (2 * PW + 2)) ** 2
    z = 1j * ALPHA * (lam[:, None] + lam[None, :])
    diag = 1.0 + z * (1.0 + z / 2.0 * (1.0 + z / 3.0 * (1.0 + z / 4.0)))
    diag = np.stack([diag.real, diag.imag]).astype(np.float32)

    def split(x):
        hi = x.astype(np.float32).astype(ml_dtypes.bfloat16)
        lo = (x - hi.astype(np.float64)).astype(np.float32).astype(ml_dtypes.bfloat16)
        return hi, lo

    both = (np.exp(1j * ang) / 16.0) @ sine

    def pair(g):
        rh, rl = split(g.real)
        ih, il = split(g.imag)
        hi = np.block([[rh, -ih], [ih, rh]])
        lo = np.block([[rl, -il], [il, rl]])
        return [hi, lo, hi.T, lo.T]

    sh, sl = split(sine)
    blocks = pair(both) + [np.concatenate([sh, sl], axis=1)]
    return diag, np.concatenate([x.astype(ml_dtypes.bfloat16) for x in blocks], axis=0)


def sincos(x):
    h = 0.5 * x
    z = h * h
    s = h * (1.0 + z * (-1 / 6 + z * (1 / 120 + z * (-1 / 5040 + z * (1 / 362880)))))
    c = 1.0 + z * (-0.5 + z * (1 / 24 + z * (-1 / 720 + z * (1 / 40320 + z * (-1 / 3628800)))))
    return 2.0 * s * c, 1.0 - 2.0 * s * s


def interleave(a, b, na, nb):
    done = units = 0
    for weight in a:
        units += weight
        while done * na < units * nb and next(b, None) is not None:
            done += 1
    for _ in b:
        pass


def run(steps):
    for _ in steps:
        pass


def compute_kernel(offs_ref, members_ref, counts_ref, obj, probe, meas, diag, table, grad,
                   a0, a1, b0, va, vb, e1, lhs, rhs, lhs_s, lhs_t, rhs_s, hb):
    lane = lax.broadcasted_iota(jnp.int32, (R, LANES), 1)
    first, last = lane == 0, lane == LANES - 1

    zero8 = jnp.zeros((PAD, LANES), jnp.float32)
    for buf in (a0.at[0], a0.at[1], b0, va, vb):
        for c in range(2):
            for h in range(2):
                buf[c, h, 0:PAD, :] = zero8
                buf[c, h, PAD + PW:, :] = zero8
    for j in range(2):
        for t in range(grad.shape[1]):
            grad[j, t] = jnp.zeros(grad.shape[2:], jnp.float32)

    def load(buf, c, h, r0):
        return buf[c, h, pl.ds(PAD + r0, R), :]

    def store(buf, c, h, r0, v):
        buf[c, h, pl.ds(PAD + r0, R), :] = v

    def lap(v, c, r0):
        mid = [load(v, c, h, r0) for h in range(2)]
        lf = [pltpu.roll(m, 1, 1) for m in mid]
        rt = [pltpu.roll(m, LANES - 1, 1) for m in mid]
        lf = [jnp.where(first, 0.0, lf[0]), jnp.where(first, lf[0], lf[1])]
        rt = [jnp.where(last, rt[1], rt[0]), jnp.where(last, 0.0, rt[1])]
        out = []
        for h in range(2):
            up = v[c, h, pl.ds(PAD + r0 - 1, R), :]
            dn = v[c, h, pl.ds(PAD + r0 + 1, R), :]
            out.append((up + dn) + (lf[h] + rt[h]) - 4.0 * mid[h])
        return out

    def step(v, u, k, r0):
        lr, li = lap(v, 0, r0), lap(v, 1, r0)
        c = ALPHA / k
        re = [load(u, 0, h, r0) - c * li[h] for h in range(2)]
        im = [load(u, 1, h, r0) + c * lr[h] for h in range(2)]
        return re, im

    def propagate(u, final):
        seq = [(u, va, 4), (va, vb, 3), (vb, va, 2)]
        for v, out, k in seq:
            for r0 in range(0, PW, R):
                re, im = step(v, u, k, r0)
                for h in range(2):
                    store(out, 0, h, r0, re[h])
                    store(out, 1, h, r0, im[h])
                yield True
        for r0 in range(0, PW, R):
            re, im = step(va, u, 1, r0)
            final(r0, re, im)
            yield True

    def split(x):
        hi = x.astype(jnp.bfloat16)
        lo = (x - hi.astype(jnp.float32)).astype(jnp.bfloat16)
        return hi, lo

    def put_lhs(r0, h, re, im):
        for c, x in enumerate((re, im)):
            hi, lo = split(x)
            lhs[pl.ds(r0, R), pl.ds(c * PW + h * LANES, LANES)] = hi
            lhs[pl.ds(r0, R), pl.ds((2 + c) * PW + h * LANES, LANES)] = lo

    def put_sine(dst, r0, h, re, im):
        for c, x in enumerate((re, im)):
            hi, lo = split(x)
            dst[pl.ds(c * PW + r0, R), pl.ds(h * LANES, LANES)] = hi
            dst[pl.ds(c * PW + r0, R), pl.ds(PW + h * LANES, LANES)] = lo

    def dot(x, y):
        return jnp.dot(x, y, preferred_element_type=jnp.float32)

    def tile(x, r0, h):
        return x[r0:r0 + R, h * LANES:(h + 1) * LANES]

    def each(fn):
        for r0 in range(0, PW, R):
            for h in range(2):
                fn(r0, h)
            yield EW

    def sine_both(src, out):
        shi, slo = table[4 * TWO:, 0:PW], table[4 * TWO:, PW:]
        for c in range(2):
            rows = pl.ds(c * PW, PW)
            y = dot(src[rows, 0:PW], shi) + dot(src[rows, PW:], shi) + dot(src[rows, 0:PW], slo)
            hi, lo = split(y)
            rhs_s[0:PW, c * PW:(c + 1) * PW] = hi
            rhs_s[PW:, c * PW:(c + 1) * PW] = lo
            yield 1
        for c in range(2):
            cols = pl.ds(c * PW, PW)
            hi, lo = rhs_s[0:PW, cols], rhs_s[PW:, cols]
            out.append(dot(shi, hi) + dot(shi, lo) + dot(slo, hi))
            yield 1

    def transform(way, out):
        left, right = 2 * TWO * way, 2 * TWO * (1 - way)
        for c in range(2):
            cols = pl.ds(c * PW, PW)
            hi, lo = table[pl.ds(right, TWO), cols], table[pl.ds(right + TWO, TWO), cols]
            y = dot(lhs[:, 0:TWO], hi) + dot(lhs[:, TWO:], hi) + dot(lhs[:, 0:TWO], lo)
            hi, lo = split(y)
            rhs[c * PW:(c + 1) * PW, :] = hi
            rhs[(2 + c) * PW:(3 + c) * PW, :] = lo
            yield 2
        for c in range(2):
            hi, lo = table[pl.ds(left + c * PW, PW), :], table[pl.ds(left + TWO + c * PW, PW), :]
            out.append(dot(hi, rhs[0:TWO, :]) + dot(hi, rhs[TWO:, :]) + dot(lo, rhs[0:TWO, :]))
            yield 2

    def times_diag(src, put, sign=1):
        def f(r0, h):
            dr, di = (diag[c, pl.ds(r0, R), pl.ds(h * LANES, LANES)] for c in range(2))
            x, y = tile(src[0], r0, h), tile(src[1], r0, h)
            put(r0, h, x * dr - sign * (y * di), x * di + sign * (y * dr))
        return each(f)

    def place(k):
        p = members_ref[0, k]
        r = offs_ref[0, p]
        col = offs_ref[1, p]
        col = jnp.where(col < 0, col + TILES * LANES, col)
        t0 = col // LANES
        return r, [lax.rem(t0 + t, TILES) for t in range(3)], col - t0 * LANES

    def times_e1(par, r0, h, re, im):
        cs = e1[par, 0, h, pl.ds(r0, R), :]
        sn = e1[par, 1, h, pl.ds(r0, R), :]
        return re * cs - im * sn, re * sn + im * cs

    def head(k, par):
        r, tiles, s = place(k)
        back = lax.rem(LANES - s + LANES, LANES)
        keep = lane < LANES - s
        u = a0.at[par]

        def window(j, r0):
            x = [pltpu.roll(obj[j, tiles[t], pl.ds(r + r0, R), :], back, 1) for t in range(3)]
            return [jnp.where(keep, x[h], x[h + 1]) for h in range(2)]

        for r0 in range(0, PW, R):
            w0, w1 = window(0, r0), window(1, r0)
            for h in range(2):
                sn, cs = sincos(w0[h])
                pr = probe[0, pl.ds(r0, R), pl.ds(h * LANES, LANES)]
                pi = probe[1, pl.ds(r0, R), pl.ds(h * LANES, LANES)]
                store(u, 0, h, r0, pr * cs - pi * sn)
                store(u, 1, h, r0, pr * sn + pi * cs)
                sn, cs = sincos(w1[h])
                e1[par, 0, h, pl.ds(r0, R), :] = cs
                e1[par, 1, h, pl.ds(r0, R), :] = sn
            yield True

        def enter(r0, re, im):
            for h in range(2):
                x, y = times_e1(par, r0, h, re[h], im[h])
                a1[par, 0, h, pl.ds(r0, R), :] = x
                a1[par, 1, h, pl.ds(r0, R), :] = y
                put_sine(lhs_s, r0, h, x, y)

        yield from propagate(u, enter)

    def middle(k):
        x = []
        yield from sine_both(lhs_s, x)
        yield from times_diag(x, put_lhs)
        far = []
        yield from transform(0, far)

        def back(r0, h):
            x, y = tile(far[0], r0, h), tile(far[1], r0, h)
            d = (4.0 * SCALE) * (x * x + y * y - meas[k, pl.ds(r0, R), pl.ds(h * LANES, LANES)])
            put_lhs(r0, h, d * x, d * y)
        yield from each(back)
        x = []
        yield from transform(1, x)
        yield from times_diag(x, functools.partial(put_sine, lhs_t), -1)
        y = []
        yield from sine_both(lhs_t, y)
        for c in range(2):
            hb[c] = y[c]
        yield 0

    def tail(k, par, valid):
        r, tiles, s = place(k)
        fwd = lax.rem(s, LANES)
        keep = lane < s
        u = a0.at[par]

        def scatter(j, r0, g):
            y = [pltpu.roll(jnp.where(valid, x, 0.0), fwd, 1) for x in g]
            vals = [jnp.where(keep, 0.0, y[0]), jnp.where(keep, y[0], y[1]), jnp.where(keep, y[1], 0.0)]
            for t in range(3):
                grad[j, tiles[t], pl.ds(r + r0, R), :] += vals[t]

        for r0 in range(0, PW, R):
            g = []
            for h in range(2):
                x, y = (hb[c, pl.ds(r0, R), pl.ds(h * LANES, LANES)] for c in range(2))
                g.append(-(x * a1[par, 1, h, pl.ds(r0, R), :] + y * a1[par, 0, h, pl.ds(r0, R), :]))
                x, y = times_e1(par, r0, h, x, y)
                store(b0, 0, h, r0, x)
                store(b0, 1, h, r0, y)
            scatter(1, r0, g)
            yield True

        def leave(r0, re, im):
            g = [-(re[h] * load(u, 1, h, r0) + im[h] * load(u, 0, h, r0)) for h in range(2)]
            scatter(0, r0, g)
        yield from propagate(b0, leave)

    count = counts_ref[0, 0]
    run(head(0, 0))

    def vector_work(i):
        other = lax.rem(i + 1, 2)
        yield from tail(jnp.maximum(i - 1, 0), other, i > 0)
        yield from head(jnp.minimum(i + 1, GMAX - 1), other)

    @pl.loop(0, count)
    def _(i):
        interleave(middle(i), vector_work(i), NA, NB)

    run(tail(count - 1, lax.rem(count - 1, 2), True))


def compute(offsets, members, counts, obj, probe, meas, *consts):
    f32, bf = jnp.float32, jnp.bfloat16
    field = pltpu.VMEM((2, 2, PW + 2 * PAD, LANES), f32)
    smem = pl.BlockSpec(memory_space=pltpu.SMEM)
    vmem = pl.BlockSpec(memory_space=pltpu.VMEM)
    return pl.pallas_call(
        compute_kernel,
        out_shape=jax.ShapeDtypeStruct(obj.shape, f32),
        in_specs=[smem] * 3 + [vmem] * 5,
        out_specs=vmem,
        scratch_shapes=[
            pltpu.VMEM((2, 2, 2, PW + 2 * PAD, LANES), f32), pltpu.VMEM((2, 2, 2, PW, LANES), f32), field, field, field,
            pltpu.VMEM((2, 2, 2, PW, LANES), f32),
            pltpu.VMEM((PW, 4 * PW), bf), pltpu.VMEM((4 * PW, PW), bf),
            pltpu.VMEM((2 * PW, 2 * PW), bf), pltpu.VMEM((2 * PW, 2 * PW), bf), pltpu.VMEM((2 * PW, 2 * PW), bf),
            pltpu.VMEM((2, PW, PW), f32),
        ],
        compiler_params=pltpu.CompilerParams(vmem_limit_bytes=24 * 1024 * 1024),
        name="slots",
    )(offsets, members, counts, obj, probe, meas, *consts)
EDGE = 128
MESH = pl.DeviceIdType.MESH
ANY = pl.BlockSpec(memory_space=pl.ANY)
VM = pl.BlockSpec(memory_space=pltpu.VMEM)


class Place:
    def __init__(self):
        self.p, self.s = lax.axis_index("probe"), lax.axis_index("strip")
        self.c = self.p % 2
        self.y = (self.p // 2) % 4
        self.z = self.p // 8

    def zz(self, d):
        return (self.z, self.z + 1 - 2 * (self.z % 2), 3 - self.z, (self.z + 2) % 4)[d]

    def yy(self, d):
        return (self.y + d + 4) % 4

    def dev(self, z=None, y=None, c=None, s=None):
        z = self.z if z is None else z
        y = self.y if y is None else y
        c = self.c if c is None else c
        return (z * 8 + y * 2 + c, self.s if s is None else s)

    def partners(self):
        return ([self.dev(y=self.yy(1)), self.dev(y=self.yy(-1)), self.dev(c=1 - self.c)]
                + [self.dev(z=self.zz(d)) for d in (1, 2, 3)]
                + [self.dev(s=(self.s + 1) % 8), self.dev(s=(self.s + 7) % 8)])

    def barrier(self):
        sem = pltpu.get_barrier_semaphore()
        partners = self.partners()
        for who in partners:
            pl.semaphore_signal(sem, inc=1, device_id=who, device_id_type=MESH)
        pl.semaphore_wait(sem, len(partners))


class Copies:
    def __init__(self, send_sems, recv_sems):
        self.ss, self.rs, self.started = send_sems, recv_sems, []

    def send(self, i, src, dst, who):
        cp = pltpu.make_async_remote_copy(src_ref=src, dst_ref=dst, send_sem=self.ss.at[i], recv_sem=self.rs.at[i],
                                          device_id=who, device_id_type=MESH)
        cp.start()
        self.started.append(cp)

    def recv(self, i, dst, who):
        pltpu.make_async_remote_copy(src_ref=dst, dst_ref=dst, send_sem=self.ss.at[i], recv_sem=self.rs.at[i],
                                     device_id=who, device_id_type=MESH).wait_recv()

    def drain(self):
        for cp in self.started:
            cp.wait_send()


MAIN, EDGES = pl.ds(0, 8), pl.ds(8, 2)


def gather_kernel(own, obj, pack, ss, rs, local_sems):
    at = Place()
    cps = Copies(ss, rs)
    tiles_in = [pltpu.make_async_copy(own.at[:, :, pl.ds(t * 128, 128)], pack.at[:, t, 0], local_sems.at[2 + t])
                for t in range(8)]
    for cp in tiles_in:
        cp.start()
    at.barrier()
    for cp in tiles_in:
        cp.wait()
    left, right = at.dev(s=(at.s + 7) % 8), at.dev(s=(at.s + 1) % 8)
    up, down, sib = at.dev(y=at.yy(1)), at.dev(y=at.yy(-1)), at.dev(c=1 - at.c)
    cps.send(53, pack.at[:, 0], pack.at[:, 8], left)
    cps.send(54, pack.at[:, 7], pack.at[:, 9], right)

    def block(n, y, c, j=None):
        js = pl.ds(0, 2) if j is None else pl.ds(j, 1)
        return obj.at[js, EDGES, pl.ds(0, 4), y, c] if n == 4 else obj.at[js, MAIN, pl.ds(at.zz(n), 1), y, c]

    def keep(i, tiles):
        cp = pltpu.make_async_copy(pack.at[:, tiles], obj.at[:, tiles, pl.ds(at.z, 1), at.y, at.c], local_sems.at[i])
        cp.start()
        return cp

    def to_z(i, tiles):
        for e in (1, 2, 3):
            cps.send(i + e, pack.at[:, tiles], obj.at[:, tiles, pl.ds(at.z, 1), at.y, at.c], at.dev(z=at.zz(e)))

    def first(n):
        dst = block(n, at.y, at.c)
        src = pack.at[:, MAIN] if n == 0 else dst
        if 0 < n < 4:
            cps.recv(45 + n, dst, at.dev(z=at.zz(n)))
        if n == 4:
            for e in (1, 2, 3):
                cps.recv(49 + e, obj.at[:, EDGES, pl.ds(at.zz(e), 1), at.y, at.c], at.dev(z=at.zz(e)))
        cps.send(n, src, dst, up)
        cps.send(5 + n, src, dst, down)
        if n == 0:
            to_z(45, MAIN)
        cps.send(20 + n, src, dst, sib)

    def second(n):
        for i, j, here, there in ((0, 0, down, up), (1, 1, up, down)):
            y = at.yy(2 * i - 1)
            got = block(n, y, at.c)
            cps.recv(5 * i + n, got, here)
            half = block(n, y, at.c, j)
            cps.send(10 + 5 * i + n, half, half, there)
            cps.send(25 + 5 * i + n, got, got, sib)

    def third(n):
        for j, who in ((0, down), (1, up)):
            half = block(n, at.yy(2), at.c, j)
            cps.recv(10 + 5 * j + n, half, who)
            cps.send(35 + 5 * j + n, half, half, sib)

    first(0)
    kept = keep(0, MAIN)
    cps.recv(53, pack.at[:, 8], right)
    cps.recv(54, pack.at[:, 9], left)

    @pl.when(at.s == 7)
    def _():
        pack[:, 8, 0] = jnp.zeros((2, 16, 128), jnp.float32)

    @pl.when(at.s == 0)
    def _():
        pack[:, 9, 0] = jnp.zeros((2, 16, 128), jnp.float32)

    to_z(49, EDGES)
    kept_edges = keep(1, EDGES)
    first(1)
    second(0)
    first(2)
    second(1)
    third(0)
    kept_edges.wait()
    first(4)
    first(3)
    second(2)
    third(1)
    second(4)
    second(3)
    third(2)
    third(4)
    third(3)
    for n in range(5):
        cps.recv(20 + n, block(n, at.y, 1 - at.c), sib)
        cps.recv(25 + n, block(n, at.yy(-1), 1 - at.c), sib)
        cps.recv(30 + n, block(n, at.yy(1), 1 - at.c), sib)
        for j in range(2):
            cps.recv(35 + 5 * j + n, block(n, at.yy(2), 1 - at.c, j), sib)
    kept.wait()
    cps.drain()


def gather(own):
    return pl.pallas_call(
        gather_kernel,
        out_shape=jax.ShapeDtypeStruct((2, 10, 4, 4, 2, 16, 128), jnp.float32),
        in_specs=[ANY],
        out_specs=ANY,
        scratch_shapes=[pltpu.VMEM((2, 10, 1, 16, 128), jnp.float32), pltpu.SemaphoreType.DMA((55,)),
                        pltpu.SemaphoreType.DMA((55,)), pltpu.SemaphoreType.DMA((10,))],
        compiler_params=pltpu.CompilerParams(collective_id=0, has_side_effects=True,
                                             vmem_limit_bytes=16 * 1024 * 1024),
        name="gather_rows",
    )(own)


def reduce_kernel(grad, out, acc, sib_in, half_in, half_e, full_in, full_e, z_in, z_e, edge_in, ss, rs, local_sems):
    at = Place()
    cps = Copies(ss, rs)
    order = (4, 3, 2, 1, 0)

    def span(n):
        return (EDGES, pl.ds(0, 4)) if n == 4 else (MAIN, pl.ds(at.zz(n), 1))

    loads = {}
    for n in order:
        ts, zs = span(n)
        loads[n] = pltpu.make_async_copy(grad.at[:, ts, zs, :, at.c], acc.at[:, ts, zs], local_sems.at[n])
        loads[n].start()
    at.barrier()
    up, down, sib = at.dev(y=at.yy(1)), at.dev(y=at.yy(-1)), at.dev(c=1 - at.c)
    left, right = at.dev(s=(at.s + 7) % 8), at.dev(s=(at.s + 1) % 8)
    for n in order:
        ts, zs = span(n)
        cps.send(n, grad.at[:, ts, zs, :, 1 - at.c], sib_in.at[:, ts, zs], sib)

    def halves(n, j):
        return half_e.at[pl.ds(j, 1)] if n == 4 else half_in.at[n, pl.ds(j, 1)]

    def fulls(n, i):
        return full_e.at[i] if n == 4 else full_in.at[n, i]

    def first(n):
        ts, zs = span(n)
        loads[n].wait()
        cps.recv(n, sib_in.at[:, ts, zs], sib)
        y = at.yy(2)
        acc[:, ts, zs, y] += sib_in[:, ts, zs, y]
        cps.send(5 + n, acc.at[0:1, ts, zs, y], halves(n, 0), up)
        cps.send(10 + n, acc.at[1:2, ts, zs, y], halves(n, 1), down)
        for e in (1, -1, 0):
            y = at.yy(e)
            acc[:, ts, zs, y] += sib_in[:, ts, zs, y]

    def second(n):
        ts, zs = span(n)
        for j, e, here, there in ((0, 1, down, up), (1, -1, up, down)):
            cps.recv(5 + 5 * j + n, halves(n, j), here)
            y = at.yy(e)
            acc[j:j + 1, ts, zs, y] += halves(n, j)[...]
            cps.send(15 + 5 * j + n, acc.at[:, ts, zs, y], fulls(n, j), there)

    def third(n):
        ts, zs = span(n)
        cps.recv(15 + n, fulls(n, 0), down)
        cps.recv(20 + n, fulls(n, 1), up)
        acc[:, ts, zs, at.y] += fulls(n, 0)[...] + fulls(n, 1)[...]
        for e in (1, 2, 3):
            if n == 4:
                cps.send(28 + e, acc.at[:, EDGES, at.zz(e), at.y], z_e.at[e - 1], at.dev(z=at.zz(e)))
            elif n == e:
                cps.send(24 + e, acc.at[:, MAIN, at.zz(e), at.y], z_in.at[e - 1], at.dev(z=at.zz(e)))

    def edges():
        for e in (1, 2, 3):
            cps.recv(28 + e, z_e.at[e - 1], at.dev(z=at.zz(e)))
        acc[:, EDGES, at.z, at.y] += (z_e[0] + z_e[1]) + z_e[2]
        cps.send(32, acc.at[:, 8, at.z, at.y], edge_in.at[0], right)
        cps.send(33, acc.at[:, 9, at.z, at.y], edge_in.at[1], left)

    first(4)
    first(3)
    second(4)
    first(2)
    second(3)
    third(4)
    first(1)
    second(2)
    third(3)
    edges()
    first(0)
    second(1)
    third(2)
    second(0)
    third(1)
    cps.recv(32, edge_in.at[0], left)
    cps.recv(33, edge_in.at[1], right)
    third(0)
    for e in (3, 2, 1):
        cps.recv(24 + e, z_in.at[e - 1], at.dev(z=at.zz(e)))
    for t in range(8):
        value = acc[:, t, at.z, at.y] + ((z_in[0, :, t] + z_in[1, :, t]) + z_in[2, :, t])
        if t == 0:
            value = value + jnp.where(at.s > 0, edge_in[0], 0.0)
        if t == 7:
            value = value + jnp.where(at.s < 7, edge_in[1], 0.0)
        out[:, :, t * 128:(t + 1) * 128] = value
    cps.drain()


def reduce_rows(grad):
    f32 = jnp.float32
    return pl.pallas_call(
        reduce_kernel,
        out_shape=jax.ShapeDtypeStruct((2, 16, 1024), f32),
        in_specs=[ANY],
        out_specs=VM,
        scratch_shapes=[pltpu.VMEM((2, 10, 4, 4, 16, 128), f32), pltpu.VMEM((2, 10, 4, 4, 16, 128), f32),
                        pltpu.VMEM((4, 2, 8, 1, 16, 128), f32), pltpu.VMEM((2, 2, 4, 16, 128), f32),
                        pltpu.VMEM((4, 2, 2, 8, 1, 16, 128), f32), pltpu.VMEM((2, 2, 2, 4, 16, 128), f32),
                        pltpu.VMEM((3, 2, 8, 16, 128), f32), pltpu.VMEM((3, 2, 2, 16, 128), f32),
                        pltpu.VMEM((2, 2, 16, 128), f32),
                        pltpu.SemaphoreType.DMA((34,)), pltpu.SemaphoreType.DMA((34,)),
                        pltpu.SemaphoreType.DMA((5,))],
        compiler_params=pltpu.CompilerParams(collective_id=1, has_side_effects=True,
                                             vmem_limit_bytes=24 * 1024 * 1024),
        name="reduce_rows",
    )(grad)


def shards(potential, probe_wave, offsets, members, counts, measured):
    obj = gather(potential).reshape(2, 10, 512, 128)
    grad = compute(offsets[0], members[0], counts, obj, probe_wave, measured[0, 0], *tables())
    return reduce_rows(grad.reshape(2, 10, 4, 4, 2, 16, 128))


def solution(mesh):
    placed = (
        P(None, "probe", "strip"),
        P(),
        P("strip", None, None),
        P("strip", "probe", None),
        P("strip", "probe"),
        P("strip", "probe", None, None, None),
    )
    return jax.shard_map(
        shards, mesh=mesh, in_specs=placed, out_specs=P(None, "probe", "strip"), check_vma=False
    )
```
